256 devices in a mesh: dp: 64 (over z, x, core), expert: 4 (over y).
Axes of the slice: x: 4, y: 4, z: 8, core: 2. Of those that a mesh axis runs over, the one named last changes fastest.
Arguments:
- tokens: bfloat16 [32768, 4096], P(('dp', 'expert')), may hold values from -6 to 6
- grad_out: bfloat16 [32768, 4096], P(('dp', 'expert')), may hold values from -6 to 6
- experts: int32 [32768, 2], P(('dp', 'expert')), may hold values from 0 to 7, all different within a row; in each aligned block of 128 rows (0 to 127, 128 to 255, ...) at most 64 rows name the same one
- gates: bfloat16 [32768, 2], P(('dp', 'expert')), may hold values from 0 to 1, as said below
- router_weight: bfloat16 [8, 4096], replicated, may hold values from -3 to 3
- saved_outputs: bfloat16 [131072, 4096], P(('dp', 'expert')), may hold values from -0.19921875 to 0.19921875
Outputs:
- input_grad: bfloat16 [32768, 4096], P(('dp', 'expert'))
- router_grad: float32 [8, 4096], replicated
- expert_grad: bfloat16 [131072, 4096], P(('dp', 'expert'))
The draws below stay inside these ranges and needn't reach their ends.
Inputs may be any that keep to these rules, and one draw needn't show every extreme that they name: Within each aligned block of 128 tokens (the tokens of one device), no expert is named by more than 64 slots, and in some blocks an expert is named by exactly 64 slots. The two experts of a token differ. The two gates of a token are positive and add up to one, up to rounding to bfloat16.
All inputs are finite; a program needn't handle non-finite values.
Results may differ from the reference program's by a relative error of at most 0.0085.
Values may be sent and summed in bfloat16 or wider, within the bound.
No kernel may reach another device: no remote copies, remote signals or barrier semaphores. Data moves between devices by JAX's collectives and lax.ppermute only.
A program may use at most 64 MiB of HBM per device.

```python
import math
import jax
import jax.numpy as jnp
import numpy as np
from jax import lax

D = 4096
TOPK = 2
TOK_DEV = 128
EXPERTS = 8
MOST = 64
TOKENS = 32768
SLOTS = 131072
N_DP = 64
N_EXPERT = 4


def draw_gates(key, part):
    leading = jax.random.uniform(key, (TOKENS, 1), jnp.float32, 0.1, 0.9)
    return jnp.concatenate([leading, 1.0 - leading], axis=1).astype(jnp.bfloat16)


def shard_levels(key, dims, split, low, high):
    gain, own = 1.0, jax.random.fold_in(key, 6)
    for dim, shards_of in split:
        steps = jnp.exp(jax.random.uniform(jax.random.fold_in(own, dim), (shards_of,), jnp.float32, low / len(split), high / len(split)))
        gain = gain * jnp.repeat(steps, dims[dim] // shards_of).reshape([-1 if axis == dim else 1 for axis in range(len(dims))])
    return gain


def assign_block(key, own, number, rows, amount, top, bound, lean):
    ranking = jax.random.permutation(key, amount)
    crowded, common = load_shares(amount, rows * top, bound, lean, True), load_shares(amount, rows * top, bound, lean, False)
    places = jnp.arange(amount)

    def named(sizes, rotation):
        used = int((sizes > 0).sum())
        fixed = max(1, used // 4)
        shifted = fixed + (places - fixed + rotation * (used - fixed)) % max(1, amount - fixed)
        return jnp.zeros((amount,), jnp.int32).at[ranking[jnp.where(places < fixed, places, shifted)]].set(jnp.asarray(sizes, jnp.int32))

    sizes = jnp.where(number % 4 == 0, named(crowded, number // 4), named(common, number - number // 4 - 1))
    mixed = jax.random.permutation(jax.random.fold_in(own, 3), amount)
    donor, receiver = mixed[0:amount // 2 * 2:2], mixed[1:amount // 2 * 2:2]
    room = jnp.minimum(sizes[donor] - 1, bound - sizes[receiver]) // 2
    room = jnp.where((donor == ranking[0]) | (receiver == ranking[0]) | (sizes[receiver] == 0), 0, jnp.maximum(room, 0))
    shifted = jax.random.randint(jax.random.fold_in(own, 4), (amount // 2,), 0, 1 << 20) % (room + 1)
    sizes = sizes.at[donor].add(-shifted).at[receiver].add(shifted)
    labels = jnp.searchsorted(jnp.cumsum(sizes), jnp.arange(rows * top), side="right").astype(jnp.int32)
    grid = labels.reshape(top, rows).T
    grid = grid[jax.random.permutation(jax.random.fold_in(own, 1), rows)]
    rotation = jax.random.randint(jax.random.fold_in(own, 2), (rows, 1), 0, top)
    return jnp.take_along_axis(grid, (jnp.arange(top)[None, :] + rotation) % top, axis=1)


def load_shares(number_of, total, bound, lean, full):
    weights = [(1 << 20) // math.isqrt(standing ** lean) + 1 for standing in range(1, number_of + 1)]
    largest = bound if full else min(bound, max(-(-total // number_of), total * weights[0] // sum(weights)))
    least = 1 if total - largest >= number_of - 1 else 0
    given, rest = [largest] + [least] * (number_of - 1), total - largest - least * (number_of - 1)
    while rest > 0:
        candidates = [i for i in range(1, number_of) if given[i] < largest] or [i for i in range(1, number_of) if given[i] < bound]
        pool, budget = sum([weights[i] for i in candidates]), rest
        for i in candidates:
            extra = min(bound - given[i], max(1, budget * weights[i] // pool), rest)
            given[i] = given[i] + extra
            rest = rest - extra
    return np.array(given)


def bell_draw(key, dims, deviation, bound, pieces=(), kind=jnp.bfloat16):
    values = jax.random.normal(key, dims, jnp.float32) * deviation
    if len(pieces) > 0:
        values = shard_levels(key, dims, pieces, -0.22, 0.18) * values
    return jnp.clip(values, min=-bound, max=bound).astype(kind)


def setup_inputs(seed: int = 0) -> dict:
    seeds = jax.random.split(jax.random.key(seed), 7)
    tokens = bell_draw(seeds[0], (TOKENS, D), 1.0, 6.0, ((0, 256),))
    grad_out = bell_draw(seeds[1], (TOKENS, D), 1.0, 6.0, ((0, 256),))
    experts_keys = jax.random.split(jax.random.fold_in(seeds[2], 1), TOKENS // TOK_DEV)
    experts_turns = jax.random.permutation(jax.random.fold_in(seeds[2], 3), TOKENS // TOK_DEV)
    experts = jax.vmap(lambda own, number: assign_block(jax.random.fold_in(seeds[2], 2), own, number, TOK_DEV, EXPERTS, TOPK, MOST, 2))(experts_keys, experts_turns).reshape((TOKENS, TOPK))
    gates = draw_gates(jax.random.fold_in(seeds[6], 71), 0)
    router_weight = bell_draw(seeds[4], (EXPERTS, D), 0.5, 3.0)
    saved_outputs = bell_draw(seeds[5], (SLOTS, D), 0.03125, 0.19921875, ((0, 256),))
    return {"tokens": tokens, "grad_out": grad_out, "experts": experts, "gates": gates, "router_weight": router_weight, "saved_outputs": saved_outputs}


def slot_positions(chosen):
    slot_expert = chosen.reshape(-1).astype(jnp.int32)
    onehot = (slot_expert[:, None] == jnp.arange(EXPERTS, dtype=jnp.int32)[None, :]).astype(jnp.int32)
    before = jnp.cumsum(onehot, axis=0) - onehot
    position = jnp.sum(before * onehot, axis=1).astype(jnp.int32)
    return slot_expert, position


def reference(tokens, grad_out, experts, gates, router_weight, saved_outputs):
    groups = N_EXPERT
    shaped = (
        tokens.reshape(N_DP, groups, TOK_DEV, D),
        grad_out.reshape(N_DP, groups, TOK_DEV, D),
        experts.reshape(N_DP, groups, TOK_DEV, TOPK),
        gates.reshape(N_DP, groups, TOK_DEV, TOPK),
        saved_outputs.reshape(N_DP, EXPERTS, groups, MOST, D),
    )

    def one_shard(inputs):
        feature, upstream, chosen, gate_raw, stored = inputs
        slot_expert, position = jax.vmap(slot_positions)(chosen)
        source = jnp.broadcast_to(jnp.arange(groups, dtype=jnp.int32)[:, None], slot_expert.shape)
        picked = stored[slot_expert, source, position]
        repeated = jnp.repeat(upstream, TOPK, axis=1)
        products = jnp.sum(repeated.astype(jnp.float32) * picked.astype(jnp.float32), axis=-1)
        gate_grad = products.reshape(groups, TOK_DEV, TOPK)
        gate_values = gate_raw.astype(jnp.float32)
        blended = jnp.sum(gate_values * gate_grad, axis=-1, keepdims=True)
        slot_grad = gate_values * (gate_grad - blended)
        onehot = (chosen[..., None] == jnp.arange(EXPERTS, dtype=jnp.int32)).astype(jnp.float32)
        logit_grad = jnp.sum(onehot * slot_grad[..., None], axis=2).astype(jnp.bfloat16)
        partial_value = jnp.einsum("ste,std->ed", logit_grad.astype(jnp.float32), feature.astype(jnp.float32))
        through = jnp.einsum("ste,ed->std", logit_grad.astype(jnp.float32), router_weight.astype(jnp.float32))
        weighted = (gate_values.reshape(groups, TOK_DEV * TOPK)[..., None] * repeated.astype(jnp.float32)).astype(jnp.bfloat16)
        scattered = jnp.zeros((EXPERTS, groups, MOST, D), jnp.bfloat16).at[slot_expert, source, position].set(weighted)
        return partial_value, through.astype(jnp.bfloat16), scattered

    partials, through, scattered = lax.map(one_shard, shaped)
    router_grad = jnp.sum(partials, axis=0) * (TOKENS ** -0.5)
    return through.reshape(TOKENS, D), router_grad, scattered.reshape(SLOTS, D)
```

```python
import functools

import jax
import jax.numpy as jnp
from jax import lax
from jax.experimental import pallas as pl
from jax.experimental.pallas import tpu as pltpu
from jax.sharding import Mesh
from jax.sharding import PartitionSpec as P

DP_EXPERT = ("dp_0", "dp_1", "dp_2", "expert")
CHUNK = 1024
BF16 = jnp.bfloat16
F32 = jnp.float32


def shift(a, step):
    n = lax.axis_size("expert")
    return lax.ppermute(a, "expert", [(i, (i + step) % n) for i in range(n)])


def prepare_kernel(me_ref, meta_ref, info_ref):
    first = 2 * me_ref[0]
    row = lax.broadcasted_iota(jnp.int32, (8, 128), 0)
    held = (first + row).astype(F32)
    earlier = lax.broadcasted_iota(jnp.int32, (128, 128), 0)
    later = lax.broadcasted_iota(jnp.int32, (128, 128), 1)
    before = jnp.where(earlier < later, 1.0, 0.0).astype(BF16)
    for s in range(meta_ref.shape[0]):
        meta = meta_ref[s]
        is0 = jnp.broadcast_to(meta[0:1], (8, 128)) == held
        is1 = jnp.broadcast_to(meta[1:2], (8, 128)) == held
        named = jnp.logical_or(is0, is1)
        count = jnp.dot(
            jnp.where(named, 1.0, 0.0).astype(BF16), before, preferred_element_type=F32
        )
        gate = jnp.where(is0, jnp.broadcast_to(meta[2:3], (8, 128)), jnp.broadcast_to(meta[3:4], (8, 128)))
        position = jnp.where(named, count, -1.0)
        info_ref[s, 0:2, :] = position[0:2]
        info_ref[s, 2:4, :] = gate[0:2]


def prepare(me, meta):
    return pl.pallas_call(
        prepare_kernel,
        out_shape=jax.ShapeDtypeStruct(meta.shape, F32),
        in_specs=[
            pl.BlockSpec(memory_space=pltpu.SMEM),
            pl.BlockSpec(memory_space=pltpu.VMEM),
        ],
        out_specs=pl.BlockSpec(memory_space=pltpu.VMEM),
    )(me, meta)


def chosen(info, h):
    slot = lax.broadcasted_iota(jnp.int32, (64, 128), 0).astype(F32)
    return slot == jnp.broadcast_to(info[h : h + 1], (64, 128))


def source_kernel(with_products, with_grad, aliased, *refs):
    refs = list(refs)
    source_ref, info_ref = refs[0], refs[1]
    at = 2
    if with_products:
        saved_ref = refs[at]
        at += 1
    upper_ref, lower_ref = refs[at], refs[at + 1]
    at += 2 + aliased
    if with_products:
        products_ref = refs[at]
        at += 1
    if with_grad:
        grad_ref = refs[at]
        at += 1
    if with_products:
        total_ref = refs[at]
        at += 1
    if with_grad:
        pick_ref = refs[at]
    step = pl.program_id(0)
    rows = jnp.concatenate([upper_ref[...], lower_ref[...]], axis=0)

    if with_grad:

        @pl.when(step == 0)
        def _():
            info = info_ref[0]
            for h in range(2):
                gate = jnp.broadcast_to(info[2 + h : 3 + h], (64, 128))
                pick_ref[64 * h : 64 * h + 64, :] = jnp.where(chosen(info, h), gate, 0.0).astype(BF16)

        scaled = jnp.dot(pick_ref[...], rows, preferred_element_type=F32).astype(BF16)
        grad_ref[0, 0] = scaled[0:64]
        grad_ref[1, 0] = scaled[64:128]

    if with_products:

        @pl.when(step == 0)
        def _():
            total_ref[...] = jnp.zeros_like(total_ref)

        stored = jnp.concatenate([saved_ref[0, 0], saved_ref[1, 0]], axis=0)
        total_ref[...] += lax.dot_general(
            stored, rows, (((1,), (1,)), ((), ())), preferred_element_type=F32
        )

        @pl.when(step == pl.num_programs(0) - 1)
        def _():
            info = info_ref[0]
            products_ref[...] = jnp.zeros_like(products_ref)
            for h in range(2):
                z = total_ref[64 * h : 64 * h + 64, :]
                products_ref[h : h + 1, :] = jnp.sum(
                    jnp.where(chosen(info, h), z, 0.0), axis=0, keepdims=True
                )


def from_source(source, info, saved, upper, lower, grad, with_products, with_grad):
    width = saved.shape[-1]
    upper, up = upper
    lower, low = lower
    grid = (width // CHUNK,)
    half = (64, CHUNK)
    in_specs = [pl.BlockSpec((1, 8, 128), lambda i, s: (s[0], 0, 0))]
    operands = [info]
    block = pl.BlockSpec((2, 1, 64, CHUNK), lambda i, s: (0, s[0], 0, i))
    if with_products:
        in_specs.append(block)
        operands.append(saved)
    in_specs += [
        pl.BlockSpec(half, lambda i, s: (up, i)),
        pl.BlockSpec(half, lambda i, s: (low, i)),
    ]
    operands += [upper, lower]
    aliased = grad is not None
    aliases = {}
    out_specs, out_shape, scratch = [], [], []
    if with_products:
        out_specs.append(pl.BlockSpec((8, 128), lambda i, s: (0, 0)))
        out_shape.append(jax.ShapeDtypeStruct((8, 128), F32))
        scratch.append(pltpu.VMEM((128, 128), F32))
    if aliased:
        in_specs.append(pl.BlockSpec(memory_space=pl.ANY))
        operands.append(grad)
        aliases = {len(operands): len(out_shape)}
    if with_grad:
        out_specs.append(block)
        out_shape.append(jax.ShapeDtypeStruct(saved.shape, BF16))
        scratch.append(pltpu.VMEM((128, 128), BF16))
    return pl.pallas_call(
        functools.partial(source_kernel, with_products, with_grad, aliased),
        grid_spec=pltpu.PrefetchScalarGridSpec(
            num_scalar_prefetch=1,
            grid=grid,
            in_specs=in_specs,
            out_specs=out_specs,
            scratch_shapes=scratch,
        ),
        out_shape=out_shape,
        input_output_aliases=aliases,
        cost_estimate=pl.CostEstimate(
            flops=4 * 128 * 128 * width, bytes_accessed=6 * 128 * width, transcendentals=0
        ),
    )(source, *operands)


def logit_kernel(me_ref, meta_ref, p0_ref, p1_ref, p2_ref, p3_ref, tokens_ref, logit_ref, part_ref):
    first = 2 * me_ref[0]
    meta = meta_ref[...]
    e0, e1, g0, g1 = meta[0:1], meta[1:2], meta[2:3], meta[3:4]
    gg0 = jnp.zeros((1, 128), F32)
    gg1 = jnp.zeros((1, 128), F32)
    for d, p_ref in enumerate((p0_ref, p1_ref, p2_ref, p3_ref)):
        for h in range(2):
            expert = lax.rem(first + 2 * d + h, 8).astype(F32)
            line = p_ref[h : h + 1, :]
            gg0 = gg0 + jnp.where(e0 == expert, line, 0.0)
            gg1 = gg1 + jnp.where(e1 == expert, line, 0.0)
    blended = g0 * gg0 + g1 * gg1
    s0 = g0 * (gg0 - blended)
    s1 = g1 * (gg1 - blended)
    row = lax.broadcasted_iota(jnp.int32, (8, 128), 0).astype(F32)
    wide = lambda v: jnp.broadcast_to(v, (8, 128))
    logit = jnp.where(wide(e0) == row, wide(s0), 0.0) + jnp.where(wide(e1) == row, wide(s1), 0.0)
    logit = logit.astype(BF16)
    logit_ref[...] = logit
    parts = part_ref.shape[0]
    piece = part_ref.shape[2]
    for j in range(parts):
        part_ref[j] = jnp.dot(
            logit, tokens_ref[:, j * piece : (j + 1) * piece], preferred_element_type=F32
        )


def logits(me, meta, products, tokens, parts):
    width = tokens.shape[1]
    vmem = pl.BlockSpec(memory_space=pltpu.VMEM)
    return pl.pallas_call(
        logit_kernel,
        out_shape=[
            jax.ShapeDtypeStruct((8, 128), BF16),
            jax.ShapeDtypeStruct((parts, 8, width // parts), F32),
        ],
        in_specs=[pl.BlockSpec(memory_space=pltpu.SMEM)] + [vmem] * 6,
        out_specs=[vmem, vmem],
    )(me, meta, *products, tokens)


def local(tokens, grad_out, experts, gates, router_weight, saved_outputs):
    width = tokens.shape[1]
    place = lax.axis_index("expert")
    groups = lax.axis_size("expert")
    me = jnp.reshape(place, (1,)).astype(jnp.int32)
    at = [lax.rem(me + d, groups) for d in range(groups)]
    saved = saved_outputs.reshape(2, groups, 64, width)
    upper, lower = grad_out[:64], grad_out[64:]

    from_left_upper = shift(upper, 1)
    from_right_lower = shift(lower, -1)
    meta = jnp.concatenate(
        [experts.astype(F32).T, gates.astype(F32).T, jnp.zeros((4, 128), F32)], axis=0
    )
    copies = jnp.broadcast_to(meta, (groups, 8, 128))
    everyone = lax.all_to_all(copies, "expert", 0, 0, tiled=True)
    info = prepare(me, everyone)
    lower_next, upper_next, info = lax.optimization_barrier((lower, upper, info))
    from_left_lower = shift(lower_next, 1)
    from_right_upper = shift(upper_next, -1)
    p_own, expert_grad = from_source(
        at[0], info, saved, (grad_out, 0), (grad_out, 1), None, True, True
    )
    far_in, near_in, p_own = lax.optimization_barrier((from_left_upper, from_right_lower, p_own))
    far_upper = shift(far_in, 1)
    far_lower = shift(near_in, -1)
    p_left, expert_grad = from_source(
        at[3], info, saved, (from_left_upper, 0), (from_left_lower, 0), expert_grad, True, True
    )
    p_right, expert_grad = from_source(
        at[1], info, saved, (from_right_upper, 0), (from_right_lower, 0), expert_grad, True, True
    )
    home_right = shift(p_left, -1)
    home_left = shift(p_right, 1)
    (p_far,) = from_source(at[2], info, saved, (far_upper, 0), (far_lower, 0), None, True, False)
    home_far = shift(p_far, 2)
    (expert_grad,) = from_source(
        at[2], info, saved, (far_upper, 0), (far_lower, 0), expert_grad, False, True
    )

    parts = lax.axis_size(("dp_2", "expert"))
    logit, partial = logits(me, meta, (p_own, home_right, home_far, home_left), tokens, parts)
    near = lax.all_to_all(partial, ("dp_2", "expert"), 0, 0, tiled=True).sum(axis=0)
    far_count = lax.axis_size(("dp_0", "dp_1"))
    copies = jnp.broadcast_to(near.astype(BF16), (far_count, *near.shape))
    total = lax.all_to_all(copies, ("dp_0", "dp_1"), 0, 0, tiled=True).astype(F32).sum(axis=0)
    scale = float(lax.axis_size(DP_EXPERT) * tokens.shape[0]) ** (-0.5)
    total = total * scale
    whole = lax.all_to_all(
        jnp.broadcast_to(total, (parts, *total.shape)), ("dp_2", "expert"), 0, 0, tiled=True
    )
    router_grad = whole.swapaxes(0, 1).reshape(8, width)
    input_grad = lax.dot_general(
        logit, router_weight, (((0,), (0,)), ((), ())), preferred_element_type=F32
    ).astype(BF16)
    return input_grad, router_grad, expert_grad.reshape(saved_outputs.shape)


def solution(mesh):
    finer = Mesh(
        mesh.devices.reshape(8, 4, 2, mesh.shape["expert"]), ("dp_0", "dp_1", "dp_2", "expert")
    )
    rows = P(DP_EXPERT, None)
    return jax.shard_map(
        local,
        mesh=finer,
        in_specs=(rows, rows, rows, rows, P(), rows),
        out_specs=(rows, P(), rows),
        check_vma=False,
    )
```

```python
import functools

import jax
import jax.numpy as jnp
from jax import lax
from jax.experimental import pallas as pl
from jax.experimental.pallas import tpu as pltpu
from jax.sharding import Mesh
from jax.sharding import PartitionSpec as P

DP_EXPERT = ("dp_0", "dp_1", "dp_2", "expert")
PLANE = ("dp_1", "dp_2")
HOUSE = ("dp_1", "dp_2", "expert")
REST = ("dp_0", "expert")
BF16 = jnp.bfloat16
F32 = jnp.float32
SMEM = pl.BlockSpec(memory_space=pltpu.SMEM)
VMEM = pl.BlockSpec(memory_space=pltpu.VMEM)
ANY = pl.BlockSpec(memory_space=pl.ANY)
PARAMS = pltpu.CompilerParams(vmem_limit_bytes=16 * 2**20)


def cost(flops, size):
    return pl.CostEstimate(flops=flops, bytes_accessed=size, transcendentals=0)


def shift(a, step, axis="expert"):
    n = lax.axis_size(axis)
    return lax.ppermute(a, axis, [(i, (i + step) % n) for i in range(n)])


def to_all(a, axes):
    return lax.all_to_all(a, axes, 0, 0, tiled=True)


def wide(v, rows=8):
    return jnp.broadcast_to(v, (rows, v.shape[1]))


def prepare_kernel(place_ref, meta_ref, info_ref):
    house, me = place_ref[0], place_ref[1]
    groups = info_ref.shape[0]
    row = lax.broadcasted_iota(jnp.int32, (8, 128), 0)
    held = (2 * me + row).astype(F32)
    earlier = lax.broadcasted_iota(jnp.int32, (128, 128), 0)
    later = lax.broadcasted_iota(jnp.int32, (128, 128), 1)
    before = jnp.where(earlier < later, 1.0, 0.0).astype(BF16)
    for s in range(groups):
        meta = meta_ref[house * groups + s]
        is0 = wide(meta[0:1]) == held
        is1 = wide(meta[1:2]) == held
        named = jnp.logical_or(is0, is1)
        count = jnp.dot(
            jnp.where(named, 1.0, 0.0).astype(BF16), before, preferred_element_type=F32
        )
        info_ref[s, 0:2, :] = jnp.where(named, count, -1.0)[0:2]
        info_ref[s, 2:4, :] = jnp.where(is0, wide(meta[2:3]), wide(meta[3:4]))[0:2]


def prepare(place, meta, groups):
    return pl.pallas_call(
        prepare_kernel,
        out_shape=jax.ShapeDtypeStruct((groups, 8, 128), F32),
        in_specs=[SMEM, VMEM],
        out_specs=VMEM,
        cost_estimate=cost(1 << 21, 1 << 17),
    )(place, meta)


def chosen(info, h):
    slot = lax.broadcasted_iota(jnp.int32, (64, 128), 0).astype(F32)
    return slot == wide(info[h : h + 1], 64)


def stacked(pieces):
    return pieces[0][...] if len(pieces) == 1 else jnp.concatenate([p[...] for p in pieces], axis=0)


def products(info, saved_ref, s, pieces):
    stored = jnp.concatenate([saved_ref[0, s], saved_ref[1, s]], axis=0)
    total = lax.dot_general(
        stored, stacked(pieces), (((1,), (1,)), ((), ())), preferred_element_type=F32
    )
    return [
        jnp.sum(jnp.where(chosen(info, h), total[64 * h : 64 * h + 64], 0.0), axis=0, keepdims=True)
        for h in range(2)
    ]


def near_kernel(place_ref, info_ref, saved_ref, own, lu, ll, ru, rl, out_ref):
    me = place_ref[1]
    groups = info_ref.shape[0]
    for d, pieces in ((0, (own,)), (1, (ru, rl)), (3, (lu, ll))):
        s = lax.rem(me + d, groups)
        for h, line in enumerate(products(info_ref[s], saved_ref, s, pieces)):
            out_ref[d, h : h + 1, :] = line


def near_products(place, info, saved, pieces):
    groups, width = info.shape[0], saved.shape[-1]
    return pl.pallas_call(
        near_kernel,
        out_shape=jax.ShapeDtypeStruct((groups, 2, 128), F32),
        in_specs=[SMEM] + [VMEM] * 7,
        out_specs=VMEM,
        compiler_params=PARAMS,
        cost_estimate=cost(6 * 128 * 128 * width, 12 * 128 * width),
    )(place, info, saved, *pieces)


def far_kernel(place_ref, info_ref, saved_ref, up, low, near_ref, out_ref):
    me = place_ref[1]
    groups = info_ref.shape[0]
    s = lax.rem(me + 2, groups)
    lines = {2: jnp.concatenate(products(info_ref[s], saved_ref, s, (up, low)), axis=0)}
    for d in (0, 1, 3):
        lines[d] = near_ref[d]
    for d in range(groups):
        t = lax.rem(me + d, groups)
        for j in range(out_ref.shape[0]):
            out_ref[j, t] = lines[d]


def far_products(place, info, saved, pieces, near, copies):
    groups, width = info.shape[0], saved.shape[-1]
    return pl.pallas_call(
        far_kernel,
        out_shape=jax.ShapeDtypeStruct((copies, groups, 2, 128), F32),
        in_specs=[SMEM] + [VMEM] * 5,
        out_specs=VMEM,
        compiler_params=PARAMS,
        cost_estimate=cost(2 * 128 * 128 * width, 4 * 128 * width),
    )(place, info, saved, *pieces, near)


def scaled_kernel(place_ref, info_ref, own, lu, ll, ru, rl, fu, fl, out_ref, pick_ref, held_ref, sems):
    me = place_ref[1]
    groups = info_ref.shape[0]
    started = []
    for d, pieces in ((0, (own,)), (1, (ru, rl)), (3, (lu, ll)), (2, (fu, fl))):
        s = lax.rem(me + d, groups)
        info = info_ref[s]
        for h in range(2):
            pick_ref[64 * h : 64 * h + 64, :] = jnp.where(
                chosen(info, h), wide(info[2 + h : 3 + h], 64), 0.0
            ).astype(BF16)
        held_ref[d] = jnp.dot(
            pick_ref[...], stacked(pieces), preferred_element_type=F32
        ).astype(BF16)
        for h in range(2):
            copy = pltpu.make_async_copy(
                held_ref.at[d, 64 * h : 64 * h + 64], out_ref.at[h, s], sems.at[2 * d + h]
            )
            copy.start()
            started.append(copy)
    for copy in started:
        copy.wait()


def scaled_rows(place, info, pieces, shape):
    groups, width = info.shape[0], shape[-1]
    return pl.pallas_call(
        scaled_kernel,
        out_shape=jax.ShapeDtypeStruct(shape, BF16),
        in_specs=[SMEM] + [VMEM] * 8,
        out_specs=ANY,
        scratch_shapes=[
            pltpu.VMEM((128, 128), BF16),
            pltpu.VMEM((groups, 128, width), BF16),
            pltpu.SemaphoreType.DMA((2 * groups,)),
        ],
        compiler_params=PARAMS,
        cost_estimate=cost(8 * 128 * 128 * width, 16 * 128 * width),
    )(place, info, *pieces)


def turn_kernel(place_ref, tokens_ref, kept_ref, sent_ref):
    column, core = place_ref[2], place_ref[3]
    columns, _, piece = kept_ref.shape
    for k in range(columns):
        first = lax.rem(column + k, columns) * 2
        for out_ref, c in ((kept_ref, core), (sent_ref, 1 - core)):
            at = pl.multiple_of((first + c) * piece, piece)
            out_ref[k] = tokens_ref[:, pl.ds(at, piece)]


def turn(place, tokens, columns):
    piece = tokens.shape[1] // (2 * columns)
    shape = jax.ShapeDtypeStruct((columns, 128, piece), BF16)
    return pl.pallas_call(
        turn_kernel,
        out_shape=[shape, shape],
        in_specs=[SMEM, VMEM],
        out_specs=[VMEM, VMEM],
        compiler_params=PARAMS,
        cost_estimate=cost(0, 4 * tokens.size),
    )(place, tokens)


def plane_blocks(kept, sent):
    columns = kept.shape[0]
    got = shift(sent, 1, "dp_2")
    blocks = [jnp.stack([kept[k], got[k]]) for k in range(columns)]
    return blocks[:1] + [shift(blocks[k], k, "dp_1") for k in range(1, columns)]


def logit_kernel(place_ref, meta_ref, home_ref, t0_ref, t1_ref, t2_ref, t3_ref, logit_ref, out_ref):
    me, column, core = place_ref[1], place_ref[2], place_ref[3]
    tokens_refs = (t0_ref, t1_ref, t2_ref, t3_ref)
    columns = len(tokens_refs)
    groups = home_ref.shape[0] // (2 * columns)
    row = lax.broadcasted_iota(jnp.int32, (8, 128), 0).astype(F32)
    part = None
    for k in range(columns):
        found = []
        for r in range(2):
            b = lax.rem(column + columns - k, columns) * 2 + lax.rem(core + r, 2)
            meta = meta_ref[b * groups + me]
            e0, e1, g0, g1 = meta[0:1], meta[1:2], meta[2:3], meta[3:4]
            grads = jnp.concatenate([home_ref[b * groups + y] for y in range(groups)], axis=0)
            is0, is1 = wide(e0) == row, wide(e1) == row
            gg0 = jnp.sum(jnp.where(is0, grads, 0.0), axis=0, keepdims=True)
            gg1 = jnp.sum(jnp.where(is1, grads, 0.0), axis=0, keepdims=True)
            blended = g0 * gg0 + g1 * gg1
            s0 = g0 * (gg0 - blended)
            s1 = g1 * (gg1 - blended)
            logit = jnp.where(is0, wide(s0), 0.0) + jnp.where(is1, wide(s1), 0.0)
            found.append(logit.astype(BF16))
        if k == 0:
            logit_ref[...] = found[0]
        features = jnp.concatenate([tokens_refs[k][0], tokens_refs[k][1]], axis=0)
        term = jnp.dot(jnp.concatenate(found, axis=1), features, preferred_element_type=F32)
        part = term if part is None else part + term
    part = part.astype(BF16)
    for j in range(out_ref.shape[0]):
        out_ref[j] = part


def logits(place, meta, home, tokens, copies):
    piece = tokens[0].shape[2]
    return pl.pallas_call(
        logit_kernel,
        out_shape=[
            jax.ShapeDtypeStruct((8, 128), BF16),
            jax.ShapeDtypeStruct((copies, 8, piece), BF16),
        ],
        in_specs=[SMEM] + [VMEM] * 6,
        out_specs=[VMEM, VMEM],
        compiler_params=PARAMS,
        cost_estimate=cost(64 * tokens[0].size, 16 * tokens[0].size),
    )(place, meta, home, *tokens)


def total_kernel(scale, parts_ref, out_ref):
    total = parts_ref[0].astype(F32)
    for j in range(1, parts_ref.shape[0]):
        total = total + parts_ref[j].astype(F32)
    total = total * scale
    for j in range(out_ref.shape[0]):
        out_ref[j] = total


def totals(scale, parts, copies):
    return pl.pallas_call(
        functools.partial(total_kernel, scale),
        out_shape=jax.ShapeDtypeStruct((copies, *parts.shape[1:]), F32),
        in_specs=[VMEM],
        out_specs=VMEM,
        cost_estimate=cost(parts.size, 4 * parts.size),
    )(parts)


def local(tokens, grad_out, experts, gates, router_weight, saved_outputs):
    width = tokens.shape[1]
    groups = lax.axis_size("expert")
    houses = lax.axis_size(PLANE)
    place = [lax.axis_index(axis) for axis in (PLANE, "expert", "dp_1", "dp_2")]
    place = jnp.stack(place).astype(jnp.int32)
    saved = saved_outputs.reshape(2, groups, 64, width)

    upper = grad_out[:64]
    left_upper = shift(upper, 1)
    again, upper = lax.optimization_barrier((grad_out, upper))
    lower = again[64:]
    right_lower = shift(lower, -1)
    meta = jnp.concatenate(
        [experts.astype(F32).T, gates.astype(F32).T, jnp.zeros((4, 128), F32)], axis=0
    )
    kept, sent = turn(place, tokens, lax.axis_size("dp_1"))
    lower, upper, sent = lax.optimization_barrier((lower, upper, sent))
    left_lower = shift(lower, 1)
    right_upper = shift(upper, -1)
    every_meta = to_all(jnp.broadcast_to(meta, (houses * groups, 8, 128)), HOUSE)
    left_upper, right_lower, every_meta = lax.optimization_barrier(
        (left_upper, right_lower, every_meta)
    )
    far_upper = shift(left_upper, 1)
    far_lower = shift(right_lower, -1)
    turned = plane_blocks(kept, sent)
    every_meta, left_lower, right_upper, turned = lax.optimization_barrier(
        (every_meta, left_lower, right_upper, turned)
    )
    info = prepare(place, every_meta, groups)

    near_pieces = (grad_out, left_upper, left_lower, right_upper, right_lower)
    near = near_products(place, info, saved, near_pieces)
    sent = far_products(place, info, saved, (far_upper, far_lower), near, houses)
    home = to_all(sent.reshape(houses * groups, 2, 128), HOUSE)
    expert_grad = scaled_rows(place, info, (*near_pieces, far_upper, far_lower), saved.shape)

    logit, parts = logits(place, every_meta, home, turned, lax.axis_size(REST))
    scale = float(lax.axis_size(DP_EXPERT) * tokens.shape[0]) ** (-0.5)
    whole = to_all(totals(scale, to_all(parts, REST), houses), PLANE)
    router_grad = whole.swapaxes(0, 1).reshape(8, width)
    input_grad = lax.dot_general(
        logit, router_weight, (((0,), (0,)), ((), ())), preferred_element_type=F32
    ).astype(BF16)
    return input_grad, router_grad, expert_grad.reshape(saved_outputs.shape)


def solution(mesh):
    finer = Mesh(
        mesh.devices.reshape(8, 4, 2, mesh.shape["expert"]), ("dp_0", "dp_1", "dp_2", "expert")
    )
    rows = P(DP_EXPERT, None)
    return jax.shard_map(
        local,
        mesh=finer,
        in_specs=(rows, rows, rows, rows, P(), rows),
        out_specs=(rows, P(), rows),
        check_vma=False,
    )
```

```python
import functools

import jax
import jax.numpy as jnp
from jax import lax
from jax.experimental import pallas as pl
from jax.experimental.pallas import tpu as pltpu
from jax.sharding import Mesh
from jax.sharding import PartitionSpec as P

DP_EXPERT = ("dp_0", "dp_1", "dp_2", "expert")
PLANE = ("dp_1", "dp_2")
HOUSE = ("dp_1", "dp_2", "expert")
REST = ("dp_0", "expert")
BF16 = jnp.bfloat16
F32 = jnp.float32
VMEM = pl.BlockSpec(memory_space=pltpu.VMEM)
ANY = pl.BlockSpec(memory_space=pl.ANY)
PARAMS = pltpu.CompilerParams(vmem_limit_bytes=16 * 2**20)


def cost(flops, size):
    return pl.CostEstimate(flops=flops, bytes_accessed=size, transcendentals=0)


def shift(a, step):
    n = lax.axis_size("expert")
    return lax.ppermute(a, "expert", [(i, (i + step) % n) for i in range(n)])


def to_all(a, axes):
    return lax.all_to_all(a, axes, 0, 0, tiled=True)


def wide(v, rows=8):
    return jnp.broadcast_to(v, (rows, v.shape[1]))


def split_kernel(grad_ref, upper_ref, lower_ref, sems):
    copies = []
    for j in range(8):
        out_ref, at = (upper_ref, 16 * j) if j < 4 else (lower_ref, 16 * (j - 4))
        copies.append(
            pltpu.make_async_copy(
                grad_ref.at[16 * j : 16 * j + 16], out_ref.at[at : at + 16], sems.at[j]
            )
        )
    for copy in copies:
        copy.start()
    for copy in copies:
        copy.wait()


def split(grad):
    half = jax.ShapeDtypeStruct((64, grad.shape[1]), grad.dtype)
    return pl.pallas_call(
        split_kernel,
        out_shape=[half, half],
        in_specs=[ANY],
        out_specs=[ANY, ANY],
        scratch_shapes=[pltpu.SemaphoreType.DMA((8,))],
        cost_estimate=cost(0, 4 * grad.size),
    )(grad)


def columns_kernel(tokens_ref, out_ref, sems):
    count, _, piece = out_ref.shape
    copies = [
        pltpu.make_async_copy(
            tokens_ref.at[:, j * piece : (j + 1) * piece], out_ref.at[j], sems.at[j]
        )
        for j in range(count)
    ]
    for copy in copies:
        copy.start()
    for copy in copies:
        copy.wait()


def columns(tokens, count):
    return pl.pallas_call(
        columns_kernel,
        out_shape=jax.ShapeDtypeStruct((count, 128, tokens.shape[1] // count), tokens.dtype),
        in_specs=[ANY],
        out_specs=ANY,
        scratch_shapes=[pltpu.SemaphoreType.DMA((count,))],
        cost_estimate=cost(0, 4 * tokens.size),
    )(tokens)


def meta_kernel(experts_ref, gates_ref, out_ref):
    meta = jnp.concatenate(
        [experts_ref[...].astype(F32), gates_ref[...].astype(F32), jnp.zeros((4, 128), F32)], axis=0
    )
    for j in range(out_ref.shape[0]):
        out_ref[j] = meta


def meta_copies(experts, gates, count):
    return pl.pallas_call(
        meta_kernel,
        out_shape=jax.ShapeDtypeStruct((count, 8, 128), F32),
        in_specs=[VMEM, VMEM],
        out_specs=VMEM,
        cost_estimate=cost(0, 4096 * count),
    )(experts.T, gates.T)


def house_index():
    return lax.axis_index("dp_1") * 2 + lax.axis_index("dp_2")


def routing(meta, me):
    row = lax.broadcasted_iota(jnp.int32, (8, 128), 0)
    held = (2 * me + row).astype(F32)
    earlier = lax.broadcasted_iota(jnp.int32, (128, 128), 0)
    later = lax.broadcasted_iota(jnp.int32, (128, 128), 1)
    before = jnp.where(earlier < later, 1.0, 0.0).astype(BF16)
    is0 = wide(meta[0:1]) == held
    is1 = wide(meta[1:2]) == held
    named = jnp.logical_or(is0, is1)
    count = jnp.dot(jnp.where(named, 1.0, 0.0).astype(BF16), before, preferred_element_type=F32)
    position = jnp.where(named, count, -1.0)
    gate = jnp.where(is0, wide(meta[2:3]), wide(meta[3:4]))
    return jnp.concatenate([position[0:2], gate[0:2], jnp.zeros((4, 128), F32)], axis=0)


def chosen(info, h):
    slot = lax.broadcasted_iota(jnp.int32, (64, 128), 0).astype(F32)
    return slot == wide(info[h : h + 1], 64)


def stacked(pieces):
    return pieces[0][...] if len(pieces) == 1 else jnp.concatenate([p[...] for p in pieces], axis=0)


def fetch(saved_ref, s, stored_ref, sems, at):
    copies = [
        pltpu.make_async_copy(
            saved_ref.at[h, s], stored_ref.at[64 * h : 64 * h + 64], sems.at[at + h]
        )
        for h in range(2)
    ]
    for copy in copies:
        copy.start()
    return copies


def products(info, stored_ref, pieces):
    total = lax.dot_general(
        stored_ref[...], stacked(pieces), (((1,), (1,)), ((), ())), preferred_element_type=F32
    )
    return [
        jnp.sum(jnp.where(chosen(info, h), total[64 * h : 64 * h + 64], 0.0), axis=0, keepdims=True)
        for h in range(2)
    ]


def near_kernel(meta_ref, saved_ref, own, lu, ll, ru, rl, info_ref, out_ref, stored_ref, sems):
    me = lax.axis_index("expert")
    groups = info_ref.shape[0]
    order = ((0, (own,)), (1, (ru, rl)), (3, (lu, ll)))
    copies = [
        fetch(saved_ref, lax.rem(me + d, groups), stored_ref.at[j], sems, 2 * j)
        for j, (d, _) in enumerate(order)
    ]
    house = house_index()
    for s in range(groups):
        info_ref[s] = routing(meta_ref[house * groups + s], me)
    for j, (d, pieces) in enumerate(order):
        for copy in copies[j]:
            copy.wait()
        info = info_ref[lax.rem(me + d, groups)]
        for h, line in enumerate(products(info, stored_ref.at[j], pieces)):
            out_ref[d, h : h + 1, :] = line
    out_ref[2] = jnp.zeros((2, 128), F32)


def near_products(meta, saved, pieces, groups):
    width = saved.shape[-1]
    return pl.pallas_call(
        near_kernel,
        out_shape=[
            jax.ShapeDtypeStruct((groups, 8, 128), F32),
            jax.ShapeDtypeStruct((groups, 2, 128), F32),
        ],
        in_specs=[VMEM, ANY] + [VMEM] * 5,
        out_specs=[VMEM, VMEM],
        scratch_shapes=[pltpu.VMEM((3, 128, width), BF16), pltpu.SemaphoreType.DMA((6,))],
        compiler_params=PARAMS,
        cost_estimate=cost(6 * 128 * 128 * width, 12 * 128 * width),
    )(meta, saved, *pieces)


def far_kernel(info_ref, saved_ref, up, low, near_ref, out_ref, stored_ref, sems):
    me = lax.axis_index("expert")
    groups = info_ref.shape[0]
    s = lax.rem(me + 2, groups)
    copies = fetch(saved_ref, s, stored_ref, sems, 0)
    for d in (0, 1, 3):
        t = lax.rem(me + d, groups)
        for j in range(out_ref.shape[0]):
            out_ref[j, t] = near_ref[d]
    for copy in copies:
        copy.wait()
    lines = jnp.concatenate(products(info_ref[s], stored_ref, (up, low)), axis=0)
    for j in range(out_ref.shape[0]):
        out_ref[j, s] = lines


def far_products(info, saved, pieces, near, copies):
    groups, width = info.shape[0], saved.shape[-1]
    return pl.pallas_call(
        far_kernel,
        out_shape=jax.ShapeDtypeStruct((copies, groups, 2, 128), F32),
        in_specs=[VMEM, ANY] + [VMEM] * 3,
        out_specs=VMEM,
        scratch_shapes=[pltpu.VMEM((128, width), BF16), pltpu.SemaphoreType.DMA((2,))],
        compiler_params=PARAMS,
        cost_estimate=cost(2 * 128 * 128 * width, 4 * 128 * width),
    )(info, saved, *pieces, near)


def scaled_kernel(info_ref, own, lu, ll, ru, rl, fu, fl, out_ref, pick_ref, held_ref, sems):
    me = lax.axis_index("expert")
    groups = info_ref.shape[0]
    started = []
    for d, pieces in ((0, (own,)), (1, (ru, rl)), (3, (lu, ll)), (2, (fu, fl))):
        s = lax.rem(me + d, groups)
        info = info_ref[s]
        for h in range(2):
            pick_ref[64 * h : 64 * h + 64, :] = jnp.where(
                chosen(info, h), wide(info[2 + h : 3 + h], 64), 0.0
            ).astype(BF16)
        held_ref[d] = jnp.dot(
            pick_ref[...], stacked(pieces), preferred_element_type=F32
        ).astype(BF16)
        for h in range(2):
            copy = pltpu.make_async_copy(
                held_ref.at[d, 64 * h : 64 * h + 64], out_ref.at[h, s], sems.at[2 * d + h]
            )
            copy.start()
            started.append(copy)
    for copy in started:
        copy.wait()


def scaled_rows(info, pieces, shape):
    groups, width = info.shape[0], shape[-1]
    return pl.pallas_call(
        scaled_kernel,
        out_shape=jax.ShapeDtypeStruct(shape, BF16),
        in_specs=[VMEM] * 8,
        out_specs=ANY,
        scratch_shapes=[
            pltpu.VMEM((128, 128), BF16),
            pltpu.VMEM((groups, 128, width), BF16),
            pltpu.SemaphoreType.DMA((2 * groups,)),
        ],
        compiler_params=PARAMS,
        cost_estimate=cost(8 * 128 * 128 * width, 16 * 128 * width),
    )(info, *pieces)


def logit_kernel(meta_ref, home_ref, tokens_ref, logit_ref, out_ref):
    house, me = house_index(), lax.axis_index("expert")
    blocks = tokens_ref.shape[0]
    groups = home_ref.shape[0] // blocks
    row = lax.broadcasted_iota(jnp.int32, (8, 128), 0).astype(F32)
    found = []
    for b in range(blocks):
        meta = meta_ref[b * groups + me]
        e0, e1, g0, g1 = meta[0:1], meta[1:2], meta[2:3], meta[3:4]
        grads = jnp.concatenate([home_ref[b * groups + y] for y in range(groups)], axis=0)
        is0, is1 = wide(e0) == row, wide(e1) == row
        gg0 = jnp.sum(jnp.where(is0, grads, 0.0), axis=0, keepdims=True)
        gg1 = jnp.sum(jnp.where(is1, grads, 0.0), axis=0, keepdims=True)
        blended = g0 * gg0 + g1 * gg1
        s0 = g0 * (gg0 - blended)
        s1 = g1 * (gg1 - blended)
        logit = jnp.where(is0, wide(s0), 0.0) + jnp.where(is1, wide(s1), 0.0)
        found.append(logit.astype(BF16))

        @pl.when(house == b)
        def _():
            logit_ref[...] = logit.astype(BF16)

    every = jnp.concatenate(found, axis=1)
    features = tokens_ref[...].reshape(blocks * 128, tokens_ref.shape[2])
    part = jnp.dot(every, features, preferred_element_type=F32).astype(BF16)
    for j in range(out_ref.shape[0]):
        out_ref[j] = part


def logits(meta, home, tokens, copies):
    piece = tokens.shape[2]
    return pl.pallas_call(
        logit_kernel,
        out_shape=[
            jax.ShapeDtypeStruct((8, 128), BF16),
            jax.ShapeDtypeStruct((copies, 8, piece), BF16),
        ],
        in_specs=[VMEM, VMEM, VMEM],
        out_specs=[VMEM, VMEM],
        compiler_params=PARAMS,
        cost_estimate=cost(16 * tokens.size, 4 * tokens.size),
    )(meta, home, tokens)


def local(tokens, grad_out, experts, gates, router_weight, saved_outputs):
    width = tokens.shape[1]
    groups = lax.axis_size("expert")
    houses = lax.axis_size(PLANE)
    saved = saved_outputs.reshape(2, groups, 64, width)

    upper, lower = split(grad_out)
    left_upper = shift(upper, 1)
    right_lower = shift(lower, -1)
    tokens, upper, lower = lax.optimization_barrier((tokens, upper, lower))
    own_columns = columns(tokens, houses)
    own_columns, upper, lower = lax.optimization_barrier((own_columns, upper, lower))
    turned = to_all(own_columns, PLANE)
    left_lower = shift(lower, 1)
    right_upper = shift(upper, -1)
    meta = meta_copies(experts, gates, houses * groups)
    left_upper, right_lower, turned, meta = lax.optimization_barrier(
        (left_upper, right_lower, turned, meta)
    )
    far_upper = shift(left_upper, 1)
    far_lower = shift(right_lower, -1)
    every_meta = to_all(meta, HOUSE)

    near_pieces = (grad_out, left_upper, left_lower, right_upper, right_lower)
    info, near = near_products(every_meta, saved, near_pieces, groups)
    sent = far_products(info, saved, (far_upper, far_lower), near, houses)
    home = to_all(sent.reshape(houses * groups, 2, 128), HOUSE)
    expert_grad = scaled_rows(info, (*near_pieces, far_upper, far_lower), saved.shape)

    logit, parts = logits(every_meta, home, turned, lax.axis_size(REST))
    scale = float(lax.axis_size(DP_EXPERT) * tokens.shape[0]) ** (-0.5)
    total = to_all(parts, REST).astype(F32).sum(axis=0) * scale
    whole = to_all(jnp.broadcast_to(total, (houses, *total.shape)), PLANE)
    router_grad = whole.swapaxes(0, 1).reshape(8, width)
    input_grad = lax.dot_general(
        logit, router_weight, (((0,), (0,)), ((), ())), preferred_element_type=F32
    ).astype(BF16)
    return input_grad, router_grad, expert_grad.reshape(saved_outputs.shape)


def solution(mesh):
    finer = Mesh(
        mesh.devices.reshape(8, 4, 2, mesh.shape["expert"]), ("dp_0", "dp_1", "dp_2", "expert")
    )
    rows = P(DP_EXPERT, None)
    return jax.shard_map(
        local,
        mesh=finer,
        in_specs=(rows, rows, rows, rows, P(), rows),
        out_specs=(rows, P(), rows),
        check_vma=False,
    )
```

```python
import functools

import jax
import jax.numpy as jnp
from jax import lax
from jax.experimental import pallas as pl
from jax.experimental.pallas import tpu as pltpu
from jax.sharding import Mesh
from jax.sharding import PartitionSpec as P

DP_EXPERT = ("dp_0", "dp_1", "dp_2", "expert")
PLANE = ("dp_1", "dp_2")
HOUSE = ("dp_1", "dp_2", "expert")
REST = ("dp_0", "expert")
BF16 = jnp.bfloat16
F32 = jnp.float32
PIECE = 512
VMEM = pl.BlockSpec(memory_space=pltpu.VMEM)
ANY = pl.BlockSpec(memory_space=pl.ANY)
PARAMS = pltpu.CompilerParams(vmem_limit_bytes=16 * 2**20)


def cost(flops, size):
    return pl.CostEstimate(flops=flops, bytes_accessed=size, transcendentals=0)


def shift(a, step):
    n = lax.axis_size("expert")
    return lax.ppermute(a, "expert", [(i, (i + step) % n) for i in range(n)])


def to_all(a, axes):
    return lax.all_to_all(a, axes, 0, 0, tiled=True)


def wide(v, rows=8):
    return jnp.broadcast_to(v, (rows, v.shape[1]))


def meta_rows(experts_ref, gates_ref):
    lines = [experts_ref[...].astype(F32), gates_ref[...].astype(F32), jnp.zeros((12, 128), F32)]
    return jnp.concatenate(lines, axis=0).astype(BF16)


def split_kernel(experts_ref, gates_ref, grad_ref, upper_ref, lower_ref, sems):
    count = grad_ref.shape[1] // PIECE
    copies = []
    for half, out_ref in enumerate((upper_ref, lower_ref)):
        for j in range(count):
            copies.append(
                pltpu.make_async_copy(
                    grad_ref.at[64 * half : 64 * half + 64, j * PIECE : (j + 1) * PIECE],
                    out_ref.at[64 * j : 64 * j + 64],
                    sems.at[count * half + j],
                )
            )
    for copy in copies:
        copy.start()
    upper_ref[64 * count : 64 * count + 16, :] = jnp.zeros((16, PIECE), BF16)
    upper_ref[64 * count : 64 * count + 16, 0:128] = meta_rows(experts_ref, gates_ref)
    for copy in copies:
        copy.wait()


def split(experts, gates, grad):
    count = grad.shape[1] // PIECE
    return pl.pallas_call(
        split_kernel,
        out_shape=[
            jax.ShapeDtypeStruct((64 * count + 16, PIECE), BF16),
            jax.ShapeDtypeStruct((64 * count, PIECE), BF16),
        ],
        in_specs=[VMEM, VMEM, ANY],
        out_specs=[VMEM, VMEM],
        scratch_shapes=[pltpu.SemaphoreType.DMA((2 * count,))],
        cost_estimate=cost(0, 4 * grad.size),
    )(experts, gates, grad)


def columns_kernel(experts_ref, gates_ref, tokens_ref, out_ref, sems):
    count, _, piece = out_ref.shape
    copies = [
        pltpu.make_async_copy(
            tokens_ref.at[:, j * piece : (j + 1) * piece], out_ref.at[j, 0:128], sems.at[j]
        )
        for j in range(count)
    ]
    for copy in copies:
        copy.start()
    meta = meta_rows(experts_ref, gates_ref)
    for j in range(count):
        out_ref[j, 128:144, :] = jnp.zeros((16, piece), BF16)
        out_ref[j, 128:144, 0:128] = meta
    for copy in copies:
        copy.wait()


def columns(experts, gates, tokens, count):
    return pl.pallas_call(
        columns_kernel,
        out_shape=jax.ShapeDtypeStruct((count, 144, tokens.shape[1] // count), tokens.dtype),
        in_specs=[VMEM, VMEM, ANY],
        out_specs=VMEM,
        scratch_shapes=[pltpu.SemaphoreType.DMA((count,))],
        cost_estimate=cost(0, 4 * tokens.size),
    )(experts, gates, tokens)


def house_index():
    return lax.axis_index("dp_1") * 2 + lax.axis_index("dp_2")


def routing(meta, me):
    meta = meta.astype(F32)
    row = lax.broadcasted_iota(jnp.int32, (8, 128), 0)
    held = (2 * me + row).astype(F32)
    earlier = lax.broadcasted_iota(jnp.int32, (128, 128), 0)
    later = lax.broadcasted_iota(jnp.int32, (128, 128), 1)
    before = jnp.where(earlier < later, 1.0, 0.0).astype(BF16)
    is0 = wide(meta[0:1]) == held
    is1 = wide(meta[1:2]) == held
    named = jnp.logical_or(is0, is1)
    count = jnp.dot(jnp.where(named, 1.0, 0.0).astype(BF16), before, preferred_element_type=F32)
    position = jnp.where(named, count, -1.0)
    gate = jnp.where(is0, wide(meta[2:3]), wide(meta[3:4]))
    return position, gate


def chosen(position, h):
    slot = lax.broadcasted_iota(jnp.int32, (64, 128), 0).astype(F32)
    return slot == wide(position[h : h + 1], 64)


def block(pieces, j):
    if len(pieces) == 1:
        return pieces[0][:, j * PIECE : (j + 1) * PIECE]
    return jnp.concatenate([p[64 * j : 64 * j + 64, :] for p in pieces], axis=0)


def products(position, saved_ref, s, pieces):
    total = jnp.zeros((128, 128), F32)
    for j in range(saved_ref.shape[3] // PIECE):
        at = slice(j * PIECE, (j + 1) * PIECE)
        stored = jnp.concatenate([saved_ref[0, s, :, at], saved_ref[1, s, :, at]], axis=0)
        total = total + lax.dot_general(
            stored, block(pieces, j), (((1,), (1,)), ((), ())), preferred_element_type=F32
        )
    lines = [
        jnp.sum(jnp.where(chosen(position, h), total[64 * h : 64 * h + 64], 0.0), axis=0, keepdims=True)
        for h in range(2)
    ]
    return jnp.concatenate(lines, axis=0)


def scale_rows(routed, pieces, s, held_ref, out_ref, sems):
    position, gate = routed
    pick = jnp.concatenate(
        [jnp.where(chosen(position, h), wide(gate[h : h + 1], 64), 0.0) for h in range(2)], axis=0
    ).astype(BF16)
    for j in range(held_ref.shape[1] // PIECE):
        held_ref[:, j * PIECE : (j + 1) * PIECE] = jnp.dot(
            pick, block(pieces, j), preferred_element_type=F32
        ).astype(BF16)
    copies = [
        pltpu.make_async_copy(held_ref.at[64 * h : 64 * h + 64], out_ref.at[h, s], sems.at[h])
        for h in range(2)
    ]
    for copy in copies:
        copy.start()
    return copies


def near_kernel(experts_ref, gates_ref, saved_ref, own, lu, ll, ru, rl, out_ref, grad_ref, held_ref, sems):
    me = lax.axis_index("expert")
    groups = saved_ref.shape[1]
    own_meta = meta_rows(experts_ref, gates_ref)
    end = ll.shape[0]
    sources = (
        (0, own_meta, (own,)),
        (1, ru[end : end + 16, 0:128], (ru, rl)),
        (3, lu[end : end + 16, 0:128], (lu, ll)),
    )
    routed = [routing(meta, me) for _, meta, _ in sources]
    out_ref[2] = jnp.zeros((2, 128), F32)
    for j, (d, _, pieces) in enumerate(sources):
        out_ref[d] = products(routed[j][0], saved_ref, lax.rem(me + d, groups), pieces)
    copies = []
    for j, (d, _, pieces) in enumerate(sources):
        copies += scale_rows(
            routed[j], pieces, lax.rem(me + d, groups), held_ref.at[j], grad_ref, sems.at[j]
        )
    for copy in copies:
        copy.wait()


def near_sources(experts, gates, saved, pieces):
    groups, width = saved.shape[1], saved.shape[3]
    return pl.pallas_call(
        near_kernel,
        out_shape=[
            jax.ShapeDtypeStruct((groups, 2, 128), F32),
            jax.ShapeDtypeStruct(saved.shape, BF16),
        ],
        in_specs=[VMEM] * 8,
        out_specs=[VMEM, ANY],
        scratch_shapes=[pltpu.VMEM((3, 128, width), BF16), pltpu.SemaphoreType.DMA((3, 2))],
        compiler_params=PARAMS,
        cost_estimate=cost(12 * 128 * 128 * width, 18 * 128 * width),
    )(experts, gates, saved, *pieces)


def far_kernel(saved_ref, up, low, near_ref, out_ref):
    me = lax.axis_index("expert")
    groups = saved_ref.shape[1]
    s = lax.rem(me + 2, groups)
    end = low.shape[0]
    position, _ = routing(up[end : end + 16, 0:128], me)
    lines = {2: products(position, saved_ref, s, (up, low))}
    for d in (0, 1, 3):
        lines[d] = near_ref[d]
    for d in range(groups):
        t = lax.rem(me + d, groups)
        for j in range(out_ref.shape[0]):
            out_ref[j, t] = lines[d]


def far_products(saved, pieces, near, copies):
    groups, width = saved.shape[1], saved.shape[3]
    return pl.pallas_call(
        far_kernel,
        out_shape=jax.ShapeDtypeStruct((copies, groups, 2, 128), F32),
        in_specs=[VMEM] * 4,
        out_specs=VMEM,
        compiler_params=PARAMS,
        cost_estimate=cost(2 * 128 * 128 * width, 4 * 128 * width),
    )(saved, *pieces, near)


def far_rows_kernel(up, low, _, grad_ref, held_ref, sems):
    me = lax.axis_index("expert")
    groups = grad_ref.shape[1]
    end = low.shape[0]
    routed = routing(up[end : end + 16, 0:128], me)
    for copy in scale_rows(routed, (up, low), lax.rem(me + 2, groups), held_ref, grad_ref, sems):
        copy.wait()


def far_rows(pieces, grad):
    width = grad.shape[3]
    return pl.pallas_call(
        far_rows_kernel,
        out_shape=jax.ShapeDtypeStruct(grad.shape, BF16),
        in_specs=[VMEM, VMEM, ANY],
        out_specs=ANY,
        scratch_shapes=[pltpu.VMEM((128, width), BF16), pltpu.SemaphoreType.DMA((2,))],
        input_output_aliases={2: 0},
        compiler_params=PARAMS,
        cost_estimate=cost(2 * 128 * 128 * width, 4 * 128 * width),
    )(*pieces, grad)


def logit_kernel(home_ref, tokens_ref, logit_ref, out_ref):
    house = house_index()
    blocks = tokens_ref.shape[0]
    groups = home_ref.shape[0] // blocks
    row = lax.broadcasted_iota(jnp.int32, (8, 128), 0).astype(F32)
    found = []
    for b in range(blocks):
        meta = tokens_ref[b, 128:144, 0:128].astype(F32)
        e0, e1, g0, g1 = meta[0:1], meta[1:2], meta[2:3], meta[3:4]
        grads = jnp.concatenate([home_ref[b * groups + y] for y in range(groups)], axis=0)
        is0, is1 = wide(e0) == row, wide(e1) == row
        gg0 = jnp.sum(jnp.where(is0, grads, 0.0), axis=0, keepdims=True)
        gg1 = jnp.sum(jnp.where(is1, grads, 0.0), axis=0, keepdims=True)
        blended = g0 * gg0 + g1 * gg1
        s0 = g0 * (gg0 - blended)
        s1 = g1 * (gg1 - blended)
        logit = jnp.where(is0, wide(s0), 0.0) + jnp.where(is1, wide(s1), 0.0)
        found.append(logit.astype(BF16))

        @pl.when(house == b)
        def _():
            logit_ref[...] = logit.astype(BF16)

    every = jnp.concatenate(found, axis=1)
    features = jnp.concatenate([tokens_ref[b, 0:128] for b in range(blocks)], axis=0)
    part = jnp.dot(every, features, preferred_element_type=F32).astype(BF16)
    for j in range(out_ref.shape[0]):
        out_ref[j] = part


def logits(home, tokens, copies):
    piece = tokens.shape[2]
    return pl.pallas_call(
        logit_kernel,
        out_shape=[
            jax.ShapeDtypeStruct((8, 128), BF16),
            jax.ShapeDtypeStruct((copies, 8, piece), BF16),
        ],
        in_specs=[VMEM, VMEM],
        out_specs=[VMEM, VMEM],
        compiler_params=PARAMS,
        cost_estimate=cost(16 * tokens.size, 4 * tokens.size),
    )(home, tokens)


def local(tokens, grad_out, experts, gates, router_weight, saved_outputs):
    width = tokens.shape[1]
    groups = lax.axis_size("expert")
    houses = lax.axis_size(PLANE)
    saved = saved_outputs.reshape(2, groups, 64, width)

    experts, gates = experts.T, gates.T

    upper, lower = split(experts, gates, grad_out)
    left_upper = shift(upper, 1)
    right_lower = shift(lower, -1)
    tokens, upper, lower = lax.optimization_barrier((tokens, upper, lower))
    own_columns = columns(experts, gates, tokens, houses)
    own_columns, upper, lower = lax.optimization_barrier((own_columns, upper, lower))
    left_lower = shift(lower, 1)
    right_upper = shift(upper, -1)
    turned = to_all(own_columns, PLANE)
    far_upper = shift(left_upper, 1)
    far_lower = shift(right_lower, -1)
    near, expert_grad = near_sources(
        experts, gates, saved, (grad_out, left_upper, left_lower, right_upper, right_lower)
    )
    sent = far_products(saved, (far_upper, far_lower), near, houses)
    sent, turned = lax.optimization_barrier((sent, turned))
    home = to_all(sent.reshape(houses * groups, 2, 128), HOUSE)
    expert_grad = far_rows((far_upper, far_lower), expert_grad)

    logit, parts = logits(home, turned, lax.axis_size(REST))
    scale = float(lax.axis_size(DP_EXPERT) * tokens.shape[0]) ** (-0.5)
    total = to_all(parts, REST).astype(F32).sum(axis=0) * scale
    whole = to_all(jnp.broadcast_to(total, (houses, *total.shape)), PLANE)
    router_grad = whole.swapaxes(0, 1).reshape(8, width)
    input_grad = lax.dot_general(
        logit, router_weight, (((0,), (0,)), ((), ())), preferred_element_type=F32
    ).astype(BF16)
    return input_grad, router_grad, expert_grad.reshape(saved_outputs.shape)


def solution(mesh):
    finer = Mesh(
        mesh.devices.reshape(8, 4, 2, mesh.shape["expert"]), ("dp_0", "dp_1", "dp_2", "expert")
    )
    rows = P(DP_EXPERT, None)
    return jax.shard_map(
        local,
        mesh=finer,
        in_specs=(rows, rows, rows, rows, P(), rows),
        out_specs=(rows, P(), rows),
        check_vma=False,
    )
```

```python
import functools

import jax
import jax.numpy as jnp
from jax import lax
from jax.experimental import pallas as pl
from jax.experimental.pallas import tpu as pltpu
from jax.sharding import Mesh
from jax.sharding import PartitionSpec as P

DP_EXPERT = ("dp_0", "dp_1", "dp_2", "expert")
PLANE = ("dp_1", "dp_2")
HOUSE = ("dp_1", "dp_2", "expert")
REST = ("expert", "dp_0")
BF16 = jnp.bfloat16
F32 = jnp.float32
PIECE = 512
VMEM = pl.BlockSpec(memory_space=pltpu.VMEM)
ANY = pl.BlockSpec(memory_space=pl.ANY)
PARAMS = pltpu.CompilerParams(vmem_limit_bytes=16 * 2**20)


def cost(flops, size):
    return pl.CostEstimate(flops=flops, bytes_accessed=size, transcendentals=0)


def shift(a, step):
    n = lax.axis_size("expert")
    return lax.ppermute(a, "expert", [(i, (i + step) % n) for i in range(n)])


def to_all(a, axes):
    return lax.all_to_all(a, axes, 0, 0, tiled=True)


def wide(v, rows=8):
    return jnp.broadcast_to(v, (rows, v.shape[1]))


def meta_rows(experts_ref, gates_ref):
    lines = [experts_ref[...].astype(F32), gates_ref[...].astype(F32), jnp.zeros((12, 128), F32)]
    return jnp.concatenate(lines, axis=0).astype(BF16)


def split_kernel(experts_ref, gates_ref, grad_ref, upper_ref, lower_ref, rows_ref, up_ref, low_ref, sems):
    count = grad_ref.shape[1] // PIECE
    arriving = [
        pltpu.make_async_copy(grad_ref.at[64 * h : 64 * h + 64], rows_ref.at[h], sems.at[0, h])
        for h in range(2)
    ]
    for copy in arriving:
        copy.start()
    halves = (up_ref, low_ref)
    end = up_ref.shape[0] - 16
    up_ref[end:, :] = jnp.zeros((16, PIECE), BF16)
    up_ref[end:, 0:128] = meta_rows(experts_ref, gates_ref)
    leaving = [
        pltpu.make_async_copy(up_ref, upper_ref, sems.at[1, 0]),
        pltpu.make_async_copy(low_ref, lower_ref, sems.at[1, 1]),
    ]
    for half in range(2):
        arriving[half].wait()
        for j in range(count):
            halves[half][64 * j : 64 * j + 64, :] = rows_ref[half, :, j * PIECE : (j + 1) * PIECE]
        leaving[half].start()
    for copy in leaving:
        copy.wait()


def split(experts, gates, grad):
    count = grad.shape[1] // PIECE
    return pl.pallas_call(
        split_kernel,
        out_shape=[
            jax.ShapeDtypeStruct((64 * count + 16, PIECE), BF16),
            jax.ShapeDtypeStruct((64 * count, PIECE), BF16),
        ],
        in_specs=[VMEM, VMEM, ANY],
        out_specs=[ANY, ANY],
        scratch_shapes=[
            pltpu.VMEM((2, 64, grad.shape[1]), BF16),
            pltpu.VMEM((64 * count + 16, PIECE), BF16),
            pltpu.VMEM((64 * count, PIECE), BF16),
            pltpu.SemaphoreType.DMA((2, 2)),
        ],
        cost_estimate=cost(0, 4 * grad.size),
    )(experts, gates, grad)


def columns_kernel(experts_ref, gates_ref, tokens_ref, out_ref, rows_ref, held_ref, sems):
    count, _, piece = out_ref.shape
    arriving = [
        pltpu.make_async_copy(tokens_ref.at[64 * h : 64 * h + 64], rows_ref.at[h], sems.at[0, h])
        for h in range(2)
    ]
    for copy in arriving:
        copy.start()
    meta = meta_rows(experts_ref, gates_ref)
    for j in range(count):
        held_ref[j, 128:144, :] = jnp.zeros((16, piece), BF16)
        held_ref[j, 128:144, 0:128] = meta
    for half in range(2):
        arriving[half].wait()
        for j in range(count):
            held_ref[j, 64 * half : 64 * half + 64] = rows_ref[half, :, j * piece : (j + 1) * piece]
    last = pltpu.make_async_copy(held_ref, out_ref, sems.at[1, 0])
    last.start()
    last.wait()


def columns(experts, gates, tokens, count):
    piece = tokens.shape[1] // count
    return pl.pallas_call(
        columns_kernel,
        out_shape=jax.ShapeDtypeStruct((count, 144, piece), tokens.dtype),
        in_specs=[VMEM, VMEM, ANY],
        out_specs=ANY,
        scratch_shapes=[
            pltpu.VMEM((2, 64, tokens.shape[1]), BF16),
            pltpu.VMEM((count, 144, piece), BF16),
            pltpu.SemaphoreType.DMA((2, 2)),
        ],
        cost_estimate=cost(0, 4 * tokens.size),
    )(experts, gates, tokens)


def house_index():
    return lax.axis_index("dp_1") * 2 + lax.axis_index("dp_2")


def routing(meta, me):
    meta = meta.astype(F32)
    row = lax.broadcasted_iota(jnp.int32, (8, 128), 0)
    held = (2 * me + row).astype(F32)
    earlier = lax.broadcasted_iota(jnp.int32, (128, 128), 0)
    later = lax.broadcasted_iota(jnp.int32, (128, 128), 1)
    before = jnp.where(earlier < later, 1.0, 0.0).astype(BF16)
    is0 = wide(meta[0:1]) == held
    is1 = wide(meta[1:2]) == held
    named = jnp.logical_or(is0, is1)
    count = jnp.dot(jnp.where(named, 1.0, 0.0).astype(BF16), before, preferred_element_type=F32)
    position = jnp.where(named, count, -1.0)
    gate = jnp.where(is0, wide(meta[2:3]), wide(meta[3:4]))
    return position, gate


def chosen(position, h):
    slot = lax.broadcasted_iota(jnp.int32, (64, 128), 0).astype(F32)
    return slot == wide(position[h : h + 1], 64)


def block(pieces, j):
    if len(pieces) == 1:
        return pieces[0][:, j * PIECE : (j + 1) * PIECE]
    return jnp.concatenate([p[64 * j : 64 * j + 64, :] for p in pieces], axis=0)


def products(position, saved_ref, s, pieces):
    total = jnp.zeros((128, 128), F32)
    for j in range(saved_ref.shape[3] // PIECE):
        at = slice(j * PIECE, (j + 1) * PIECE)
        stored = jnp.concatenate([saved_ref[0, s, :, at], saved_ref[1, s, :, at]], axis=0)
        total = total + lax.dot_general(
            stored, block(pieces, j), (((1,), (1,)), ((), ())), preferred_element_type=F32
        )
    lines = [
        jnp.sum(jnp.where(chosen(position, h), total[64 * h : 64 * h + 64], 0.0), axis=0, keepdims=True)
        for h in range(2)
    ]
    return jnp.concatenate(lines, axis=0)


def scale_rows(routed, pieces, s, held_ref, out_ref, sems):
    position, gate = routed
    pick = jnp.concatenate(
        [jnp.where(chosen(position, h), wide(gate[h : h + 1], 64), 0.0) for h in range(2)], axis=0
    ).astype(BF16)
    for j in range(held_ref.shape[1] // PIECE):
        held_ref[:, j * PIECE : (j + 1) * PIECE] = jnp.dot(
            pick, block(pieces, j), preferred_element_type=F32
        ).astype(BF16)
    copies = [
        pltpu.make_async_copy(held_ref.at[64 * h : 64 * h + 64], out_ref.at[h, s], sems.at[h])
        for h in range(2)
    ]
    for copy in copies:
        copy.start()
    return copies


def near_kernel(experts_ref, gates_ref, saved_ref, own, lu, ll, ru, rl, out_ref, grad_ref, held_ref, sems):
    me = lax.axis_index("expert")
    groups = saved_ref.shape[1]
    own_meta = meta_rows(experts_ref, gates_ref)
    end = ll.shape[0]
    sources = (
        (0, own_meta, (own,)),
        (1, ru[end : end + 16, 0:128], (ru, rl)),
        (3, lu[end : end + 16, 0:128], (lu, ll)),
    )
    routed = [routing(meta, me) for _, meta, _ in sources]
    out_ref[2] = jnp.zeros((2, 128), F32)
    for j, (d, _, pieces) in enumerate(sources):
        out_ref[d] = products(routed[j][0], saved_ref, lax.rem(me + d, groups), pieces)
    copies = []
    for j, (d, _, pieces) in enumerate(sources):
        copies += scale_rows(
            routed[j], pieces, lax.rem(me + d, groups), held_ref.at[j], grad_ref, sems.at[j]
        )
    for copy in copies:
        copy.wait()


def near_sources(experts, gates, saved, pieces):
    groups, width = saved.shape[1], saved.shape[3]
    return pl.pallas_call(
        near_kernel,
        out_shape=[
            jax.ShapeDtypeStruct((groups, 2, 128), F32),
            jax.ShapeDtypeStruct(saved.shape, BF16),
        ],
        in_specs=[VMEM] * 8,
        out_specs=[VMEM, ANY],
        scratch_shapes=[pltpu.VMEM((3, 128, width), BF16), pltpu.SemaphoreType.DMA((3, 2))],
        compiler_params=PARAMS,
        cost_estimate=cost(12 * 128 * 128 * width, 18 * 128 * width),
    )(experts, gates, saved, *pieces)


def far_kernel(saved_ref, up, low, near_ref, out_ref):
    me = lax.axis_index("expert")
    groups = saved_ref.shape[1]
    s = lax.rem(me + 2, groups)
    end = low.shape[0]
    position, _ = routing(up[end : end + 16, 0:128], me)
    lines = {2: products(position, saved_ref, s, (up, low))}
    for d in (0, 1, 3):
        lines[d] = near_ref[d]
    for d in range(groups):
        t = lax.rem(me + d, groups)
        for j in range(out_ref.shape[0]):
            out_ref[j, t] = lines[d]


def far_products(saved, pieces, near, copies):
    groups, width = saved.shape[1], saved.shape[3]
    return pl.pallas_call(
        far_kernel,
        out_shape=jax.ShapeDtypeStruct((copies, groups, 2, 128), F32),
        in_specs=[VMEM] * 4,
        out_specs=VMEM,
        compiler_params=PARAMS,
        cost_estimate=cost(2 * 128 * 128 * width, 4 * 128 * width),
    )(saved, *pieces, near)


def far_rows_kernel(up, low, _, grad_ref, held_ref, sems):
    me = lax.axis_index("expert")
    groups = grad_ref.shape[1]
    end = low.shape[0]
    routed = routing(up[end : end + 16, 0:128], me)
    for copy in scale_rows(routed, (up, low), lax.rem(me + 2, groups), held_ref, grad_ref, sems):
        copy.wait()


def far_rows(pieces, grad):
    width = grad.shape[3]
    return pl.pallas_call(
        far_rows_kernel,
        out_shape=jax.ShapeDtypeStruct(grad.shape, BF16),
        in_specs=[VMEM, VMEM, ANY],
        out_specs=ANY,
        scratch_shapes=[pltpu.VMEM((128, width), BF16), pltpu.SemaphoreType.DMA((2,))],
        input_output_aliases={2: 0},
        compiler_params=PARAMS,
        cost_estimate=cost(2 * 128 * 128 * width, 4 * 128 * width),
    )(*pieces, grad)


def logit_kernel(home_ref, tokens_ref, logit_ref, out_ref):
    house = house_index()
    blocks = tokens_ref.shape[0]
    groups = home_ref.shape[0] // blocks
    row = lax.broadcasted_iota(jnp.int32, (8, 128), 0).astype(F32)
    found = []
    for b in range(blocks):
        meta = tokens_ref[b, 128:144, 0:128].astype(F32)
        e0, e1, g0, g1 = meta[0:1], meta[1:2], meta[2:3], meta[3:4]
        grads = jnp.concatenate([home_ref[b * groups + y] for y in range(groups)], axis=0)
        is0, is1 = wide(e0) == row, wide(e1) == row
        gg0 = jnp.sum(jnp.where(is0, grads, 0.0), axis=0, keepdims=True)
        gg1 = jnp.sum(jnp.where(is1, grads, 0.0), axis=0, keepdims=True)
        blended = g0 * gg0 + g1 * gg1
        s0 = g0 * (gg0 - blended)
        s1 = g1 * (gg1 - blended)
        logit = jnp.where(is0, wide(s0), 0.0) + jnp.where(is1, wide(s1), 0.0)
        found.append(logit.astype(BF16))

        @pl.when(house == b)
        def _():
            logit_ref[...] = logit.astype(BF16)

    every = jnp.concatenate(found, axis=1)
    features = jnp.concatenate([tokens_ref[b, 0:128] for b in range(blocks)], axis=0)
    part = jnp.dot(every, features, preferred_element_type=F32).astype(BF16)
    for j in range(out_ref.shape[0]):
        out_ref[j] = part


def logits(home, tokens, copies):
    piece = tokens.shape[2]
    return pl.pallas_call(
        logit_kernel,
        out_shape=[
            jax.ShapeDtypeStruct((8, 128), BF16),
            jax.ShapeDtypeStruct((copies, 8, piece), BF16),
        ],
        in_specs=[VMEM, VMEM],
        out_specs=[VMEM, VMEM],
        compiler_params=PARAMS,
        cost_estimate=cost(16 * tokens.size, 4 * tokens.size),
    )(home, tokens)


def local(tokens, grad_out, experts, gates, router_weight, saved_outputs):
    width = tokens.shape[1]
    groups = lax.axis_size("expert")
    houses = lax.axis_size(PLANE)
    saved = saved_outputs.reshape(2, groups, 64, width)

    experts, gates = experts.T, gates.T

    upper, lower = split(experts, gates, grad_out)
    left_upper = shift(upper, 1)
    right_lower = shift(lower, -1)
    tokens, upper, lower = lax.optimization_barrier((tokens, upper, lower))
    own_columns = columns(experts, gates, tokens, houses)
    left_lower = shift(lower, 1)
    right_upper = shift(upper, -1)
    turned = to_all(own_columns, PLANE)
    far_upper = shift(left_upper, 1)
    far_lower = shift(right_lower, -1)
    near, expert_grad = near_sources(
        experts, gates, saved, (grad_out, left_upper, left_lower, right_upper, right_lower)
    )
    sent = far_products(saved, (far_upper, far_lower), near, houses)
    sent, turned = lax.optimization_barrier((sent, turned))
    home = to_all(sent.reshape(houses * groups, 2, 128), HOUSE)
    expert_grad = far_rows((far_upper, far_lower), expert_grad)

    home, expert_grad = lax.optimization_barrier((home, expert_grad))
    logit, parts = logits(home, turned, lax.axis_size(REST))
    input_grad = lax.dot_general(
        logit, router_weight, (((0,), (0,)), ((), ())), preferred_element_type=F32
    ).astype(BF16)
    scale = float(lax.axis_size(DP_EXPERT) * tokens.shape[0]) ** (-0.5)
    total = to_all(parts, REST).astype(F32).sum(axis=0) * scale
    total, input_grad = lax.optimization_barrier((total, input_grad))
    whole = to_all(jnp.broadcast_to(total.astype(BF16), (houses, *total.shape)), PLANE).astype(F32)
    router_grad = whole.swapaxes(0, 1).reshape(8, width)
    return input_grad, router_grad, expert_grad.reshape(saved_outputs.shape)


def solution(mesh):
    finer = Mesh(
        mesh.devices.reshape(8, 4, 2, mesh.shape["expert"]), ("dp_0", "dp_1", "dp_2", "expert")
    )
    rows = P(DP_EXPERT, None)
    return jax.shard_map(
        local,
        mesh=finer,
        in_specs=(rows, rows, rows, rows, P(), rows),
        out_specs=(rows, P(), rows),
        check_vma=False,
    )
```

```python
import functools

import jax
import jax.numpy as jnp
from jax import lax
from jax.experimental import pallas as pl
from jax.experimental.pallas import tpu as pltpu
from jax.sharding import Mesh
from jax.sharding import PartitionSpec as P

DP_EXPERT = ("far_z", "near_z", "dp_1", "dp_2", "expert")
PLANE = ("dp_1", "dp_2")
HOUSE = ("dp_1", "dp_2", "expert")
REST = ("expert", "far_z", "near_z")
SLICES = ("dp_1", "dp_2", "near_z")
BF16 = jnp.bfloat16
F32 = jnp.float32
PIECE = 512
VMEM = pl.BlockSpec(memory_space=pltpu.VMEM)
ANY = pl.BlockSpec(memory_space=pl.ANY)
PARAMS = pltpu.CompilerParams(vmem_limit_bytes=16 * 2**20)


def cost(flops, size):
    return pl.CostEstimate(flops=flops, bytes_accessed=size, transcendentals=0)


def shift(a, step):
    n = lax.axis_size("expert")
    return lax.ppermute(a, "expert", [(i, (i + step) % n) for i in range(n)])


def to_all(a, axes):
    return lax.all_to_all(a, axes, 0, 0, tiled=True)


def wide(v, rows=8):
    return jnp.broadcast_to(v, (rows, v.shape[1]))


def meta_rows(experts, gates):
    lines = [experts.astype(F32), gates.astype(F32), jnp.zeros((12, 128), F32)]
    return jnp.concatenate(lines, axis=0).astype(BF16)


def fetch(pairs, sems):
    copies = [pltpu.make_async_copy(a, b, sems.at[i]) for i, (a, b) in enumerate(pairs)]
    for copy in copies:
        copy.start()
    return copies


def split_kernel(experts_hbm, gates_hbm, grad_ref, upper_ref, lower_ref, rows_ref, up_ref, low_ref, experts_ref, gates_ref, in_sems, out_sems):
    count = grad_ref.shape[1] // PIECE
    pairs = [(grad_ref.at[64 * h : 64 * h + 64], rows_ref.at[h]) for h in range(2)]
    pairs += [(experts_hbm, experts_ref), (gates_hbm, gates_ref)]
    arriving = fetch(pairs, in_sems)
    halves = (up_ref, low_ref)
    end = up_ref.shape[0] - 16
    up_ref[end:, :] = jnp.zeros((16, PIECE), BF16)
    arriving[2].wait()
    arriving[3].wait()
    up_ref[end:, 0:128] = meta_rows(experts_ref[...], gates_ref[...])
    leaving = [
        pltpu.make_async_copy(up_ref, upper_ref, out_sems.at[0]),
        pltpu.make_async_copy(low_ref, lower_ref, out_sems.at[1]),
    ]
    for half in range(2):
        arriving[half].wait()
        for j in range(count):
            halves[half][64 * j : 64 * j + 64, :] = rows_ref[half, :, j * PIECE : (j + 1) * PIECE]
        leaving[half].start()
    for copy in leaving:
        copy.wait()


def split(experts, gates, grad):
    count = grad.shape[1] // PIECE
    return pl.pallas_call(
        split_kernel,
        out_shape=[
            jax.ShapeDtypeStruct((64 * count + 16, PIECE), BF16),
            jax.ShapeDtypeStruct((64 * count, PIECE), BF16),
        ],
        in_specs=[ANY, ANY, ANY],
        out_specs=[ANY, ANY],
        scratch_shapes=[
            pltpu.VMEM((2, 64, grad.shape[1]), BF16),
            pltpu.VMEM((64 * count + 16, PIECE), BF16),
            pltpu.VMEM((64 * count, PIECE), BF16),
            pltpu.VMEM(experts.shape, experts.dtype),
            pltpu.VMEM(gates.shape, gates.dtype),
            pltpu.SemaphoreType.DMA((4,)),
            pltpu.SemaphoreType.DMA((2,)),
        ],
        cost_estimate=cost(0, 4 * grad.size),
    )(experts, gates, grad)


def columns_kernel(experts_ref, gates_ref, tokens_ref, out_ref, rows_ref, held_ref, in_sems, out_sem):
    count, _, piece = out_ref.shape
    arriving = fetch([(tokens_ref.at[64 * h : 64 * h + 64], rows_ref.at[h]) for h in range(2)], in_sems)
    meta = meta_rows(experts_ref[...], gates_ref[...])
    for j in range(count):
        held_ref[j, 128:144, :] = jnp.zeros((16, piece), BF16)
        held_ref[j, 128:144, 0:128] = meta
    for half in range(2):
        arriving[half].wait()
        for j in range(count):
            held_ref[j, 64 * half : 64 * half + 64] = rows_ref[half, :, j * piece : (j + 1) * piece]
    last = pltpu.make_async_copy(held_ref, out_ref, out_sem)
    last.start()
    last.wait()


def columns(experts, gates, tokens, count):
    piece = tokens.shape[1] // count
    return pl.pallas_call(
        columns_kernel,
        out_shape=jax.ShapeDtypeStruct((count, 144, piece), tokens.dtype),
        in_specs=[VMEM, VMEM, ANY],
        out_specs=ANY,
        scratch_shapes=[
            pltpu.VMEM((2, 64, tokens.shape[1]), BF16),
            pltpu.VMEM((count, 144, piece), BF16),
            pltpu.SemaphoreType.DMA((2,)),
            pltpu.SemaphoreType.DMA,
        ],
        cost_estimate=cost(0, 4 * tokens.size),
    )(experts, gates, tokens)


def house_index():
    return lax.axis_index("dp_1") * 2 + lax.axis_index("dp_2")


def routing(meta, me):
    meta = meta.astype(F32)
    row = lax.broadcasted_iota(jnp.int32, (8, 128), 0)
    held = (2 * me + row).astype(F32)
    earlier = lax.broadcasted_iota(jnp.int32, (128, 128), 0)
    later = lax.broadcasted_iota(jnp.int32, (128, 128), 1)
    before = jnp.where(earlier < later, 1.0, 0.0).astype(BF16)
    is0 = wide(meta[0:1]) == held
    is1 = wide(meta[1:2]) == held
    named = jnp.logical_or(is0, is1)
    count = jnp.dot(jnp.where(named, 1.0, 0.0).astype(BF16), before, preferred_element_type=F32)
    position = jnp.where(named, count, -1.0)
    gate = jnp.where(is0, wide(meta[2:3]), wide(meta[3:4]))
    return position, gate


def chosen(position, h):
    slot = lax.broadcasted_iota(jnp.int32, (64, 128), 0).astype(F32)
    return slot == wide(position[h : h + 1], 64)


def block(pieces, j):
    if len(pieces) == 1:
        return pieces[0][:, j * PIECE : (j + 1) * PIECE]
    return jnp.concatenate([p[64 * j : 64 * j + 64, :] for p in pieces], axis=0)


def products(position, saved_ref, s, pieces):
    total = jnp.zeros((128, 128), F32)
    for j in range(saved_ref.shape[3] // PIECE):
        at = slice(j * PIECE, (j + 1) * PIECE)
        stored = jnp.concatenate([saved_ref[0, s, :, at], saved_ref[1, s, :, at]], axis=0)
        total = total + lax.dot_general(
            stored, block(pieces, j), (((1,), (1,)), ((), ())), preferred_element_type=F32
        )
    lines = [
        jnp.sum(jnp.where(chosen(position, h), total[64 * h : 64 * h + 64], 0.0), axis=0, keepdims=True)
        for h in range(2)
    ]
    return jnp.concatenate(lines, axis=0)


def scale_rows(routed, pieces, s, held_ref, out_ref, sems):
    position, gate = routed
    pick = jnp.concatenate(
        [jnp.where(chosen(position, h), wide(gate[h : h + 1], 64), 0.0) for h in range(2)], axis=0
    ).astype(BF16)
    for j in range(held_ref.shape[1] // PIECE):
        held_ref[:, j * PIECE : (j + 1) * PIECE] = jnp.dot(
            pick, block(pieces, j), preferred_element_type=F32
        ).astype(BF16)
    copies = [
        pltpu.make_async_copy(held_ref.at[64 * h : 64 * h + 64], out_ref.at[h, s], sems.at[h])
        for h in range(2)
    ]
    for copy in copies:
        copy.start()
    return copies


def near_kernel(experts_ref, gates_ref, saved_ref, own, lu, ll, ru, rl, out_ref, grad_ref, held_ref, sems):
    me = lax.axis_index("expert")
    groups = saved_ref.shape[1]
    own_meta = meta_rows(experts_ref[...], gates_ref[...])
    end = ll.shape[0]
    sources = (
        (0, own_meta, (own,)),
        (1, ru[end : end + 16, 0:128], (ru, rl)),
        (3, lu[end : end + 16, 0:128], (lu, ll)),
    )
    routed = [routing(meta, me) for _, meta, _ in sources]
    out_ref[2] = jnp.zeros((2, 128), F32)
    for j, (d, _, pieces) in enumerate(sources):
        out_ref[d] = products(routed[j][0], saved_ref, lax.rem(me + d, groups), pieces)
    copies = []
    for j, (d, _, pieces) in enumerate(sources):
        copies += scale_rows(
            routed[j], pieces, lax.rem(me + d, groups), held_ref.at[j], grad_ref, sems.at[j]
        )
    for copy in copies:
        copy.wait()


def near_sources(experts, gates, saved, pieces):
    groups, width = saved.shape[1], saved.shape[3]
    return pl.pallas_call(
        near_kernel,
        out_shape=[
            jax.ShapeDtypeStruct((groups, 2, 128), F32),
            jax.ShapeDtypeStruct(saved.shape, BF16),
        ],
        in_specs=[VMEM] * 8,
        out_specs=[VMEM, ANY],
        scratch_shapes=[pltpu.VMEM((3, 128, width), BF16), pltpu.SemaphoreType.DMA((3, 2))],
        compiler_params=PARAMS,
        cost_estimate=cost(12 * 128 * 128 * width, 18 * 128 * width),
    )(experts, gates, saved, *pieces)


def far_kernel(saved_ref, up, low, near_ref, out_ref):
    me = lax.axis_index("expert")
    groups = saved_ref.shape[1]
    s = lax.rem(me + 2, groups)
    end = low.shape[0]
    position, _ = routing(up[end : end + 16, 0:128], me)
    lines = {2: products(position, saved_ref, s, (up, low))}
    for d in (0, 1, 3):
        lines[d] = near_ref[d]
    for d in range(groups):
        t = lax.rem(me + d, groups)
        for j in range(out_ref.shape[0]):
            out_ref[j, t] = lines[d]


def far_products(saved, pieces, near, copies):
    groups, width = saved.shape[1], saved.shape[3]
    return pl.pallas_call(
        far_kernel,
        out_shape=jax.ShapeDtypeStruct((copies, groups, 2, 128), F32),
        in_specs=[VMEM] * 4,
        out_specs=VMEM,
        compiler_params=PARAMS,
        cost_estimate=cost(2 * 128 * 128 * width, 4 * 128 * width),
    )(saved, *pieces, near)


def far_rows_kernel(up, low, _, grad_ref, held_ref, sems):
    me = lax.axis_index("expert")
    groups = grad_ref.shape[1]
    end = low.shape[0]
    routed = routing(up[end : end + 16, 0:128], me)
    for copy in scale_rows(routed, (up, low), lax.rem(me + 2, groups), held_ref, grad_ref, sems):
        copy.wait()


def far_rows(pieces, grad):
    width = grad.shape[3]
    return pl.pallas_call(
        far_rows_kernel,
        out_shape=jax.ShapeDtypeStruct(grad.shape, BF16),
        in_specs=[VMEM, VMEM, ANY],
        out_specs=ANY,
        scratch_shapes=[pltpu.VMEM((128, width), BF16), pltpu.SemaphoreType.DMA((2,))],
        input_output_aliases={2: 0},
        compiler_params=PARAMS,
        cost_estimate=cost(2 * 128 * 128 * width, 4 * 128 * width),
    )(*pieces, grad)


def logit_kernel(home_ref, tokens_ref, logit_ref, out_ref):
    house = house_index()
    blocks = tokens_ref.shape[0]
    groups = home_ref.shape[0] // blocks
    row = lax.broadcasted_iota(jnp.int32, (8, 128), 0).astype(F32)
    found = []
    for b in range(blocks):
        meta = tokens_ref[b, 128:144, 0:128].astype(F32)
        e0, e1, g0, g1 = meta[0:1], meta[1:2], meta[2:3], meta[3:4]
        grads = jnp.concatenate([home_ref[b * groups + y] for y in range(groups)], axis=0)
        is0, is1 = wide(e0) == row, wide(e1) == row
        gg0 = jnp.sum(jnp.where(is0, grads, 0.0), axis=0, keepdims=True)
        gg1 = jnp.sum(jnp.where(is1, grads, 0.0), axis=0, keepdims=True)
        blended = g0 * gg0 + g1 * gg1
        s0 = g0 * (gg0 - blended)
        s1 = g1 * (gg1 - blended)
        logit = jnp.where(is0, wide(s0), 0.0) + jnp.where(is1, wide(s1), 0.0)
        found.append(logit.astype(BF16))

        @pl.when(house == b)
        def _():
            logit_ref[...] = logit.astype(BF16)

    every = jnp.concatenate(found, axis=1)
    features = jnp.concatenate([tokens_ref[b, 0:128] for b in range(blocks)], axis=0)
    part = jnp.dot(every, features, preferred_element_type=F32).astype(BF16)
    piece = out_ref.shape[2]
    for j in range(out_ref.shape[0]):
        at = j % (part.shape[1] // piece) * piece
        out_ref[j] = part[:, at : at + piece]


def logits(home, tokens, copies, slices):
    piece = tokens.shape[2] // slices
    return pl.pallas_call(
        logit_kernel,
        out_shape=[
            jax.ShapeDtypeStruct((8, 128), BF16),
            jax.ShapeDtypeStruct((copies, 8, piece), BF16),
        ],
        in_specs=[VMEM, VMEM],
        out_specs=[VMEM, VMEM],
        compiler_params=PARAMS,
        cost_estimate=cost(16 * tokens.size, 4 * tokens.size),
    )(home, tokens)


def local(tokens, grad_out, experts, gates, router_weight, saved_outputs):
    width = tokens.shape[1]
    groups = lax.axis_size("expert")
    houses = lax.axis_size(PLANE)
    saved = saved_outputs.reshape(2, groups, 64, width)

    experts, gates = experts.T, gates.T

    upper, lower = split(experts, gates, grad_out)
    left_upper = shift(upper, 1)
    right_lower = shift(lower, -1)
    tokens, upper, lower = lax.optimization_barrier((tokens, upper, lower))
    own_columns = columns(experts, gates, tokens, houses)
    left_lower = shift(lower, 1)
    right_upper = shift(upper, -1)
    turned = to_all(own_columns, PLANE)
    far_upper = shift(left_upper, 1)
    far_lower = shift(right_lower, -1)
    near, expert_grad = near_sources(
        experts, gates, saved, (grad_out, left_upper, left_lower, right_upper, right_lower)
    )
    sent = far_products(saved, (far_upper, far_lower), near, houses)
    sent, turned = lax.optimization_barrier((sent, turned))
    home = to_all(sent.reshape(houses * groups, 2, 128), HOUSE)
    expert_grad = far_rows((far_upper, far_lower), expert_grad)

    logit, parts = logits(home, turned, lax.axis_size(REST), lax.axis_size("near_z"))
    input_grad = lax.dot_general(
        logit, router_weight, (((0,), (0,)), ((), ())), preferred_element_type=F32
    ).astype(BF16)
    scale = float(lax.axis_size(DP_EXPERT) * tokens.shape[0]) ** (-0.5)
    total = to_all(parts, REST).astype(F32).sum(axis=0) * scale
    total, input_grad, expert_grad = lax.optimization_barrier((total, input_grad, expert_grad))
    copies = jnp.broadcast_to(total.astype(BF16), (lax.axis_size(SLICES), *total.shape))
    whole = to_all(copies, SLICES).astype(F32)
    router_grad = whole.swapaxes(0, 1).reshape(8, width)
    return input_grad, router_grad, expert_grad.reshape(saved_outputs.shape)


def solution(mesh):
    finer = Mesh(
        mesh.devices.reshape(4, 2, 4, 2, mesh.shape["expert"]), DP_EXPERT
    )
    rows = P(DP_EXPERT, None)
    return jax.shard_map(
        local,
        mesh=finer,
        in_specs=(rows, rows, rows, rows, P(), rows),
        out_specs=(rows, P(), rows),
        check_vma=False,
    )
```

```python
import functools

import jax
import jax.numpy as jnp
from jax import lax
from jax.experimental import pallas as pl
from jax.experimental.pallas import tpu as pltpu
from jax.sharding import Mesh
from jax.sharding import PartitionSpec as P

DP_EXPERT = ("far_z", "near_z", "dp_1", "dp_2", "expert")
PLANE = ("dp_1", "dp_2")
HOUSE = ("dp_1", "dp_2", "expert")
REST = ("expert", "far_z", "near_z")
SLICES = ("dp_1", "dp_2", "near_z")
BF16 = jnp.bfloat16
F32 = jnp.float32
PIECE = 512
VMEM = pl.BlockSpec(memory_space=pltpu.VMEM)
ANY = pl.BlockSpec(memory_space=pl.ANY)
PARAMS = pltpu.CompilerParams(vmem_limit_bytes=16 * 2**20)


def cost(flops, size):
    return pl.CostEstimate(flops=flops, bytes_accessed=size, transcendentals=0)


def shift(a, step):
    n = lax.axis_size("expert")
    return lax.ppermute(a, "expert", [(i, (i + step) % n) for i in range(n)])


def to_all(a, axes):
    return lax.all_to_all(a, axes, 0, 0, tiled=True)


def wide(v, rows=8):
    return jnp.broadcast_to(v, (rows, v.shape[1]))


def meta_rows(experts, gates):
    lines = [experts.astype(F32), gates.astype(F32), jnp.zeros((12, 128), F32)]
    return jnp.concatenate(lines, axis=0).astype(BF16)


def fetch(pairs, sems):
    copies = [pltpu.make_async_copy(a, b, sems.at[i]) for i, (a, b) in enumerate(pairs)]
    for copy in copies:
        copy.start()
    return copies


def split_kernel(experts_hbm, gates_hbm, grad_ref, upper_ref, lower_ref, rows_ref, up_ref, low_ref, experts_ref, gates_ref, in_sems, out_sems):
    count = grad_ref.shape[1] // PIECE
    part = grad_ref.shape[1] // 2
    parts = [(h, q) for h in range(2) for q in range(2)]
    pairs = [
        (
            grad_ref.at[64 * h : 64 * h + 64, q * part : (q + 1) * part],
            rows_ref.at[h, :, q * part : (q + 1) * part],
        )
        for h, q in parts
    ]
    pairs += [(experts_hbm, experts_ref), (gates_hbm, gates_ref)]
    arriving = fetch(pairs, in_sems)
    halves, targets = (up_ref, low_ref), (upper_ref, lower_ref)
    end = up_ref.shape[0] - 16
    up_ref[end:, :] = jnp.zeros((16, PIECE), BF16)
    arriving[4].wait()
    arriving[5].wait()
    up_ref[end:, 0:128] = meta_rows(experts_ref[...], gates_ref[...])
    leaving = []
    for i, (h, q) in enumerate(parts):
        arriving[i].wait()
        for j in range(q * count // 2, (q + 1) * count // 2):
            halves[h][64 * j : 64 * j + 64, :] = rows_ref[h, :, j * PIECE : (j + 1) * PIECE]
        last = halves[h].shape[0] if q else 32 * count
        at = slice(32 * count * q, last)
        copy = pltpu.make_async_copy(halves[h].at[at], targets[h].at[at], out_sems.at[i])
        copy.start()
        leaving.append(copy)
    for copy in leaving:
        copy.wait()


def split(experts, gates, grad):
    count = grad.shape[1] // PIECE
    return pl.pallas_call(
        split_kernel,
        out_shape=[
            jax.ShapeDtypeStruct((64 * count + 16, PIECE), BF16),
            jax.ShapeDtypeStruct((64 * count, PIECE), BF16),
        ],
        in_specs=[ANY, ANY, ANY],
        out_specs=[ANY, ANY],
        scratch_shapes=[
            pltpu.VMEM((2, 64, grad.shape[1]), BF16),
            pltpu.VMEM((64 * count + 16, PIECE), BF16),
            pltpu.VMEM((64 * count, PIECE), BF16),
            pltpu.VMEM(experts.shape, experts.dtype),
            pltpu.VMEM(gates.shape, gates.dtype),
            pltpu.SemaphoreType.DMA((6,)),
            pltpu.SemaphoreType.DMA((4,)),
        ],
        cost_estimate=cost(0, 4 * grad.size),
    )(experts, gates, grad)


def columns_kernel(experts_ref, gates_ref, tokens_ref, out_ref, rows_ref, held_ref, in_sems, out_sem):
    count, _, piece = out_ref.shape
    arriving = fetch([(tokens_ref.at[64 * h : 64 * h + 64], rows_ref.at[h]) for h in range(2)], in_sems)
    meta = meta_rows(experts_ref[...], gates_ref[...])
    for j in range(count):
        held_ref[j, 128:144, :] = jnp.zeros((16, piece), BF16)
        held_ref[j, 128:144, 0:128] = meta
    for half in range(2):
        arriving[half].wait()
        for j in range(count):
            held_ref[j, 64 * half : 64 * half + 64] = rows_ref[half, :, j * piece : (j + 1) * piece]
    last = pltpu.make_async_copy(held_ref, out_ref, out_sem)
    last.start()
    last.wait()


def columns(experts, gates, tokens, count):
    piece = tokens.shape[1] // count
    return pl.pallas_call(
        columns_kernel,
        out_shape=jax.ShapeDtypeStruct((count, 144, piece), tokens.dtype),
        in_specs=[VMEM, VMEM, ANY],
        out_specs=ANY,
        scratch_shapes=[
            pltpu.VMEM((2, 64, tokens.shape[1]), BF16),
            pltpu.VMEM((count, 144, piece), BF16),
            pltpu.SemaphoreType.DMA((2,)),
            pltpu.SemaphoreType.DMA,
        ],
        cost_estimate=cost(0, 4 * tokens.size),
    )(experts, gates, tokens)


def house_index():
    return lax.axis_index("dp_1") * 2 + lax.axis_index("dp_2")


def routing(meta, me):
    meta = meta.astype(F32)
    row = lax.broadcasted_iota(jnp.int32, (8, 128), 0)
    held = (2 * me + row).astype(F32)
    earlier = lax.broadcasted_iota(jnp.int32, (128, 128), 0)
    later = lax.broadcasted_iota(jnp.int32, (128, 128), 1)
    before = jnp.where(earlier < later, 1.0, 0.0).astype(BF16)
    is0 = wide(meta[0:1]) == held
    is1 = wide(meta[1:2]) == held
    named = jnp.logical_or(is0, is1)
    count = jnp.dot(jnp.where(named, 1.0, 0.0).astype(BF16), before, preferred_element_type=F32)
    position = jnp.where(named, count, -1.0)
    gate = jnp.where(is0, wide(meta[2:3]), wide(meta[3:4]))
    return position, gate


def chosen(position, h):
    slot = lax.broadcasted_iota(jnp.int32, (64, 128), 0).astype(F32)
    return slot == wide(position[h : h + 1], 64)


def block(pieces, j):
    if len(pieces) == 1:
        return pieces[0][:, j * PIECE : (j + 1) * PIECE]
    return jnp.concatenate([p[64 * j : 64 * j + 64, :] for p in pieces], axis=0)


def products(position, saved_ref, s, pieces):
    total = jnp.zeros((128, 128), F32)
    for j in range(saved_ref.shape[3] // PIECE):
        at = slice(j * PIECE, (j + 1) * PIECE)
        stored = jnp.concatenate([saved_ref[0, s, :, at], saved_ref[1, s, :, at]], axis=0)
        total = total + lax.dot_general(
            stored, block(pieces, j), (((1,), (1,)), ((), ())), preferred_element_type=F32
        )
    lines = [
        jnp.sum(jnp.where(chosen(position, h), total[64 * h : 64 * h + 64], 0.0), axis=0, keepdims=True)
        for h in range(2)
    ]
    return jnp.concatenate(lines, axis=0)


def scale_rows(routed, pieces, s, held_ref, out_ref, sems):
    position, gate = routed
    pick = jnp.concatenate(
        [jnp.where(chosen(position, h), wide(gate[h : h + 1], 64), 0.0) for h in range(2)], axis=0
    ).astype(BF16)
    for j in range(held_ref.shape[1] // PIECE):
        held_ref[:, j * PIECE : (j + 1) * PIECE] = jnp.dot(
            pick, block(pieces, j), preferred_element_type=F32
        ).astype(BF16)
    copies = [
        pltpu.make_async_copy(held_ref.at[64 * h : 64 * h + 64], out_ref.at[h, s], sems.at[h])
        for h in range(2)
    ]
    for copy in copies:
        copy.start()
    return copies


def near_kernel(experts_ref, gates_ref, saved_ref, own, lu, ll, ru, rl, out_ref, grad_ref, held_ref, sems):
    me = lax.axis_index("expert")
    groups = saved_ref.shape[1]
    own_meta = meta_rows(experts_ref[...], gates_ref[...])
    end = ll.shape[0]
    sources = (
        (0, own_meta, (own,)),
        (1, ru[end : end + 16, 0:128], (ru, rl)),
        (3, lu[end : end + 16, 0:128], (lu, ll)),
    )
    routed = [routing(meta, me) for _, meta, _ in sources]
    out_ref[2] = jnp.zeros((2, 128), F32)
    for j, (d, _, pieces) in enumerate(sources):
        out_ref[d] = products(routed[j][0], saved_ref, lax.rem(me + d, groups), pieces)
    copies = []
    for j, (d, _, pieces) in enumerate(sources):
        copies += scale_rows(
            routed[j], pieces, lax.rem(me + d, groups), held_ref.at[j], grad_ref, sems.at[j]
        )
    for copy in copies:
        copy.wait()


def near_sources(experts, gates, saved, pieces):
    groups, width = saved.shape[1], saved.shape[3]
    return pl.pallas_call(
        near_kernel,
        out_shape=[
            jax.ShapeDtypeStruct((groups, 2, 128), F32),
            jax.ShapeDtypeStruct(saved.shape, BF16),
        ],
        in_specs=[VMEM] * 8,
        out_specs=[VMEM, ANY],
        scratch_shapes=[pltpu.VMEM((3, 128, width), BF16), pltpu.SemaphoreType.DMA((3, 2))],
        compiler_params=PARAMS,
        cost_estimate=cost(12 * 128 * 128 * width, 18 * 128 * width),
    )(experts, gates, saved, *pieces)


def far_kernel(saved_ref, up, low, near_ref, out_ref):
    me = lax.axis_index("expert")
    groups = saved_ref.shape[1]
    s = lax.rem(me + 2, groups)
    end = low.shape[0]
    position, _ = routing(up[end : end + 16, 0:128], me)
    lines = {2: products(position, saved_ref, s, (up, low))}
    for d in (0, 1, 3):
        lines[d] = near_ref[d]
    for d in range(groups):
        t = lax.rem(me + d, groups)
        for j in range(out_ref.shape[0]):
            out_ref[j, t] = lines[d]


def far_products(saved, pieces, near, copies):
    groups, width = saved.shape[1], saved.shape[3]
    return pl.pallas_call(
        far_kernel,
        out_shape=jax.ShapeDtypeStruct((copies, groups, 2, 128), F32),
        in_specs=[VMEM] * 4,
        out_specs=VMEM,
        compiler_params=PARAMS,
        cost_estimate=cost(2 * 128 * 128 * width, 4 * 128 * width),
    )(saved, *pieces, near)


def far_rows_kernel(up, low, _, grad_ref, held_ref, sems):
    me = lax.axis_index("expert")
    groups = grad_ref.shape[1]
    end = low.shape[0]
    routed = routing(up[end : end + 16, 0:128], me)
    for copy in scale_rows(routed, (up, low), lax.rem(me + 2, groups), held_ref, grad_ref, sems):
        copy.wait()


def far_rows(pieces, grad):
    width = grad.shape[3]
    return pl.pallas_call(
        far_rows_kernel,
        out_shape=jax.ShapeDtypeStruct(grad.shape, BF16),
        in_specs=[VMEM, VMEM, ANY],
        out_specs=ANY,
        scratch_shapes=[pltpu.VMEM((128, width), BF16), pltpu.SemaphoreType.DMA((2,))],
        input_output_aliases={2: 0},
        compiler_params=PARAMS,
        cost_estimate=cost(2 * 128 * 128 * width, 4 * 128 * width),
    )(*pieces, grad)


def logit_kernel(home_ref, tokens_ref, logit_ref, out_ref):
    house = house_index()
    blocks = tokens_ref.shape[0]
    groups = home_ref.shape[0] // blocks
    row = lax.broadcasted_iota(jnp.int32, (8, 128), 0).astype(F32)
    found = []
    for b in range(blocks):
        meta = tokens_ref[b, 128:144, 0:128].astype(F32)
        e0, e1, g0, g1 = meta[0:1], meta[1:2], meta[2:3], meta[3:4]
        grads = jnp.concatenate([home_ref[b * groups + y] for y in range(groups)], axis=0)
        is0, is1 = wide(e0) == row, wide(e1) == row
        gg0 = jnp.sum(jnp.where(is0, grads, 0.0), axis=0, keepdims=True)
        gg1 = jnp.sum(jnp.where(is1, grads, 0.0), axis=0, keepdims=True)
        blended = g0 * gg0 + g1 * gg1
        s0 = g0 * (gg0 - blended)
        s1 = g1 * (gg1 - blended)
        logit = jnp.where(is0, wide(s0), 0.0) + jnp.where(is1, wide(s1), 0.0)
        found.append(logit.astype(BF16))

        @pl.when(house == b)
        def _():
            logit_ref[...] = logit.astype(BF16)

    part = jnp.zeros((8, tokens_ref.shape[2]), F32)
    for b in range(0, blocks, 2):
        pair = jnp.concatenate([tokens_ref[b, 0:128], tokens_ref[b + 1, 0:128]], axis=0)
        part = part + jnp.dot(
            jnp.concatenate(found[b : b + 2], axis=1), pair, preferred_element_type=F32
        )
    part = part.astype(BF16)
    piece = out_ref.shape[2]
    for j in range(out_ref.shape[0]):
        at = j % (part.shape[1] // piece) * piece
        out_ref[j] = part[:, at : at + piece]


def logits(home, tokens, copies, slices):
    piece = tokens.shape[2] // slices
    return pl.pallas_call(
        logit_kernel,
        out_shape=[
            jax.ShapeDtypeStruct((8, 128), BF16),
            jax.ShapeDtypeStruct((copies, 8, piece), BF16),
        ],
        in_specs=[VMEM, VMEM],
        out_specs=[VMEM, VMEM],
        compiler_params=PARAMS,
        cost_estimate=cost(16 * tokens.size, 4 * tokens.size),
    )(home, tokens)


def local(tokens, grad_out, experts, gates, router_weight, saved_outputs):
    width = tokens.shape[1]
    groups = lax.axis_size("expert")
    houses = lax.axis_size(PLANE)
    saved = saved_outputs.reshape(2, groups, 64, width)

    experts, gates = experts.T, gates.T

    upper, lower = split(experts, gates, grad_out)
    left_upper = shift(upper, 1)
    right_lower = shift(lower, -1)
    tokens, upper, lower = lax.optimization_barrier((tokens, upper, lower))
    own_columns = columns(experts, gates, tokens, houses)
    left_lower = shift(lower, 1)
    right_upper = shift(upper, -1)
    turned = to_all(own_columns, PLANE)
    far_upper = shift(left_upper, 1)
    far_lower = shift(right_lower, -1)
    near, expert_grad = near_sources(
        experts, gates, saved, (grad_out, left_upper, left_lower, right_upper, right_lower)
    )
    sent = far_products(saved, (far_upper, far_lower), near, houses)
    sent, turned = lax.optimization_barrier((sent, turned))
    home = to_all(sent.reshape(houses * groups, 2, 128), HOUSE)
    expert_grad = far_rows((far_upper, far_lower), expert_grad)

    logit, parts = logits(home, turned, lax.axis_size(REST), lax.axis_size("near_z"))
    input_grad = lax.dot_general(
        logit, router_weight, (((0,), (0,)), ((), ())), preferred_element_type=F32
    ).astype(BF16)
    scale = float(lax.axis_size(DP_EXPERT) * tokens.shape[0]) ** (-0.5)
    total = to_all(parts, REST).astype(F32).sum(axis=0) * scale
    total, input_grad, expert_grad = lax.optimization_barrier((total, input_grad, expert_grad))
    copies = jnp.broadcast_to(total.astype(BF16), (lax.axis_size(SLICES), *total.shape))
    whole = to_all(copies, SLICES).astype(F32)
    router_grad = whole.swapaxes(0, 1).reshape(8, width)
    return input_grad, router_grad, expert_grad.reshape(saved_outputs.shape)


def solution(mesh):
    finer = Mesh(
        mesh.devices.reshape(4, 2, 4, 2, mesh.shape["expert"]), DP_EXPERT
    )
    rows = P(DP_EXPERT, None)
    return jax.shard_map(
        local,
        mesh=finer,
        in_specs=(rows, rows, rows, rows, P(), rows),
        out_specs=(rows, P(), rows),
        check_vma=False,
    )
```
